512 devices in a mesh: pop: 16 (over x, y_hi), tp: 32 (over z, y_lo, core).
Axes of the slice: x: 4, y: 8 (y_hi: 4, y_lo: 2; y = y_hi * 2 + y_lo), z: 8, core: 2. Of those that a mesh axis runs over, the one named last changes fastest.
Arguments:
- states: bfloat16 [256, 5120], P(None, 'pop'), may hold values from -6 to 6
- token_ids: int32 [640, 4], replicated, may hold values from 0 to 255
- gate_matrix: bfloat16 [5120, 16384], P('pop', 'tp'), may hold values from -0.078125 to 0.078125
- up_matrix: bfloat16 [5120, 16384], P('pop', 'tp'), may hold values from -0.078125 to 0.078125
- down_matrix: bfloat16 [16384, 5120], P('tp', 'pop'), may hold values from -0.046875 to 0.046875
- gate_left: bfloat16 [640, 5120], P(None, 'pop'), may hold values from -6 to 6
- gate_right: bfloat16 [640, 16384], P('pop', 'tp'), may hold values from -6 to 6
- up_left: bfloat16 [640, 5120], P(None, 'pop'), may hold values from -6 to 6
- up_right: bfloat16 [640, 16384], P('pop', 'tp'), may hold values from -6 to 6
- down_left: bfloat16 [640, 16384], P('pop', 'tp'), may hold values from -6 to 6
- down_right: bfloat16 [640, 5120], P(None, 'pop'), may hold values from -6 to 6
- target: bfloat16 [2560, 5120], P('tp', 'pop'), may hold values from -4 to 4
Outputs:
- layer_out: float32 [2560, 5120], P('tp', 'pop')
- gate_update: float32 [5120, 16384], P('pop', 'tp')
- up_update: float32 [5120, 16384], P('pop', 'tp')
- down_update: float32 [16384, 5120], P('tp', 'pop')
The draws below stay inside these ranges and needn't reach their ends.
All inputs are finite; a program needn't handle non-finite values.
Results may differ from the reference program's by a relative error of at most 0.0029.
Values may be sent and summed in bfloat16 or wider, within the bound.
No kernel may reach another device: no remote copies, remote signals or barrier semaphores. Data moves between devices by JAX's collectives and lax.ppermute only.
A program may use at most 128 MiB of HBM per device.

```python
import math
import jax
import jax.numpy as jnp
from jax import lax

D = 5120
FF = 16384
TPM = 4
BANK = 256
MEMBERS = 640
ROWS = 2560


def draw_target(key, part):
    key = jax.random.fold_in(key, 7)
    first, second, third = jax.random.split(key, 3)
    jitter = 0.5 * jnp.clip(jax.random.normal(first, (ROWS, D), jnp.float32), -4.0, 4.0)
    row_factor = jnp.exp(jax.random.uniform(second, (ROWS, 1), jnp.float32, -0.2, 0.2))
    column = jnp.exp(jax.random.uniform(third, (1, D), jnp.float32, jnp.log(2.0 / 3.0), jnp.log(1.5)))
    return (jitter * row_factor * column).astype(jnp.bfloat16)


def with_ends(entries, rng, low, high):
    extent = entries.shape
    place = [jax.random.randint(jax.random.fold_in(rng, axis), (), 0, extent[axis]) for axis in range(len(extent))]
    entries = entries.at[tuple(place)].set(low)
    longest = extent.index(max(extent))
    place[longest] = (place[longest] + 1) % extent[longest]
    return entries.at[tuple(place)].set(high)


def block_scale(key, dims, cuts, low, top_value):
    def one(axis_at, parts):
        steps = jax.random.uniform(jax.random.fold_in(jax.random.fold_in(key, 6), axis_at), (parts,), jnp.float32, low / len(cuts), top_value / len(cuts))
        return jnp.repeat(jnp.exp(steps), dims[axis_at] // parts).reshape((-1,) + (1,) * (len(dims) - axis_at - 1))

    factor_of = one(*cuts[0])
    for cut in cuts[1:]:
        factor_of = factor_of * one(*cut)
    return factor_of


def noise(rng, shape, width, most, cuts=(), kind=jnp.bfloat16):
    entries = width * jax.random.normal(rng, shape, jnp.float32)
    if cuts:
        entries = entries * block_scale(rng, shape, cuts, -0.22, 0.18)
    return jnp.clip(entries, -most, most).astype(kind)


def setup_inputs(seed: int = 0) -> dict:
    key_of = jax.random.split(jax.random.key(seed), 13)
    return {
        "states": noise(key_of[0], (BANK, D), 1.0, 6.0, ((1, 16),)),
        "token_ids": with_ends(jax.random.randint(key_of[1], (MEMBERS, TPM), 0, BANK), jax.random.fold_in(key_of[1], 1), 0, BANK - 1).astype(jnp.int32),
        "gate_matrix": noise(key_of[2], (D, FF), D ** -0.5, 0.078125, ((0, 16), (1, 32))),
        "up_matrix": noise(key_of[3], (D, FF), D ** -0.5, 0.078125, ((0, 16), (1, 32))),
        "down_matrix": noise(key_of[4], (FF, D), FF ** -0.5, 0.046875, ((0, 32), (1, 16))),
        "gate_left": noise(key_of[5], (MEMBERS, D), 1.0, 6.0, ((1, 16),)),
        "gate_right": noise(key_of[6], (MEMBERS, FF), 1.0, 6.0, ((0, 16), (1, 32))),
        "up_left": noise(key_of[7], (MEMBERS, D), 1.0, 6.0, ((1, 16),)),
        "up_right": noise(key_of[8], (MEMBERS, FF), 1.0, 6.0, ((0, 16), (1, 32))),
        "down_left": noise(key_of[9], (MEMBERS, FF), 1.0, 6.0, ((0, 16), (1, 32))),
        "down_right": noise(key_of[10], (MEMBERS, D), 1.0, 6.0, ((1, 16),)),
        "target": draw_target(jax.random.fold_in(key_of[12], 71), 0),
    }


spread = 0.5
epsilon = 1e-06

def outer_sum(left, right):
    return lax.dot_general(left, right, (((0,), (0,)), ((), ())), precision=lax.Precision.HIGHEST, preferred_element_type=jnp.float32)

def reference(states, token_ids, gate_matrix, up_matrix, down_matrix, gate_left, gate_right, up_left, up_right, down_left, down_right, target):
    flat_ids = token_ids.reshape(-1)
    picked = jnp.take(states, flat_ids, axis=0).astype(jnp.float32).reshape(MEMBERS, TPM, D)
    gate_base = jnp.dot(states, gate_matrix, preferred_element_type=jnp.float32)
    up_base = jnp.dot(states, up_matrix, preferred_element_type=jnp.float32)
    gate_dot = jnp.einsum('mjd,md->mj', picked, gate_left.astype(jnp.float32)) * (1.0 / math.sqrt(D))
    up_dot = jnp.einsum('mjd,md->mj', picked, up_left.astype(jnp.float32)) * (1.0 / math.sqrt(D))
    gate_pre = jnp.take(gate_base, flat_ids, axis=0).reshape(MEMBERS, TPM, FF) + spread * gate_dot[:, :, None] * gate_right.astype(jnp.float32)[:, None, :]
    up_pre = jnp.take(up_base, flat_ids, axis=0).reshape(MEMBERS, TPM, FF) + spread * up_dot[:, :, None] * up_right.astype(jnp.float32)[:, None, :]
    hidden = (jax.nn.silu(gate_pre) * up_pre).astype(jnp.bfloat16)
    down_dot = jnp.einsum('mjf,mf->mj', hidden.astype(jnp.float32), down_left.astype(jnp.float32)) * (1.0 / math.sqrt(FF))
    hidden_flat = hidden.reshape(ROWS, FF)
    summed = jnp.dot(hidden_flat, down_matrix, preferred_element_type=jnp.float32)
    raw_out = summed.reshape(MEMBERS, TPM, D) + spread * down_dot[:, :, None] * down_right.astype(jnp.float32)[:, None, :]
    layer_out = raw_out.reshape(ROWS, D)
    error = raw_out - target.astype(jnp.float32).reshape(MEMBERS, TPM, D)
    losses = lax.optimization_barrier(jnp.sum(error * error, axis=(1, 2))) / (TPM * D)
    mean_loss = jnp.mean(losses)
    spread_loss = jnp.mean((losses - mean_loss) ** 2)
    weights = -(losses - mean_loss) / jnp.sqrt(spread_loss + epsilon) * (1.0 / math.sqrt(MEMBERS))
    gate_scaled = weights[:, None] * gate_left.astype(jnp.float32)
    up_scaled = weights[:, None] * up_left.astype(jnp.float32)
    down_scaled = weights[:, None] * down_right.astype(jnp.float32)
    gate_update = outer_sum(gate_scaled, gate_right.astype(jnp.float32))
    up_update = outer_sum(up_scaled, up_right.astype(jnp.float32))
    down_update = outer_sum(down_left.astype(jnp.float32), down_scaled)
    return (layer_out, gate_update, up_update, down_update)
```

```python
import math

import jax
import jax.numpy as jnp
from jax import lax
from jax.experimental import pallas as pl
from jax.experimental.pallas import tpu as pltpu
from jax.sharding import Mesh, PartitionSpec as P

D = 5120
FF = 16384
MEMBERS = 640
TOKENS = 4
ROWS = MEMBERS * TOKENS
BANK = 256

spread = 0.5
epsilon = 1e-06

f32 = jnp.float32
bf16 = jnp.bfloat16

NX, NYH, NZ, NYL, NC = 4, 4, 8, 2, 2
POP = ("x", "yh")
TP = ("z", "yl", "c")
EVERY = POP + TP
GROUP = MEMBERS // (NX * NYH)
UNITS = 512
OWN = UNITS // (NX * NYH)
WIDTH = D // (NX * NYH)
X_ROWS = ROWS // NX
X_MEMBERS = MEMBERS // NX
BLOCK = ROWS // (NZ * NYL * NC)
BLOCK_MEMBERS = BLOCK // TOKENS
PADDED = 384


def position(x, yh, z, yl, c):
    return (((x * NYH + yh) * NZ + z) * NYL + yl) * NC + c


def to_owner():
    pairs = []
    for x in range(NX):
        for yh in range(NYH):
            for z in range(NZ):
                for yl in range(NYL):
                    for c in range(NC):
                        column, row = yl * NC + c, x * NZ + z
                        pairs.append((position(x, yh, z, yl, c), position(column, yh, 0, 0, 0) + row))
    return pairs


def split_three(value):
    high = value.astype(bf16)
    rest = value - high.astype(f32)
    middle = rest.astype(bf16)
    low = (rest - middle.astype(f32)).astype(bf16)
    return high, middle, low


def hidden_kernel(ids_ref, base_ref, dots_ref, rights_ref, out_ref):
    step = 128 * TOKENS
    scale = f32(1.0 / math.sqrt(D))
    base = jnp.concatenate(split_three(base_ref[...]), axis=0)
    repeat = (
        lax.broadcasted_iota(jnp.int32, (128, step), 1) // TOKENS
        == lax.broadcasted_iota(jnp.int32, (128, step), 0)
    ).astype(f32).astype(bf16)
    token = lax.broadcasted_iota(jnp.int32, (1, step), 1) % TOKENS
    for part in range(MEMBERS // 128):
        members = slice(part * 128, (part + 1) * 128)
        rows = slice(part * step, (part + 1) * step)
        chosen = (
            lax.broadcasted_iota(jnp.int32, (BANK, step), 0) == ids_ref[:, rows]
        ).astype(f32).astype(bf16)
        picked = jnp.dot(base, chosen, preferred_element_type=f32)
        picked = picked[: 2 * OWN] + picked[2 * OWN : 4 * OWN] + picked[4 * OWN :]
        dots = jnp.concatenate(split_three(dots_ref[:, members]), axis=0)
        dots = jnp.dot(dots, repeat, preferred_element_type=f32)
        dots = (dots[:8] + dots[8:16] + dots[16:]) * scale
        right = jnp.dot(rights_ref[:, members], repeat, preferred_element_type=f32)
        gate_dot = jnp.zeros((1, step), f32)
        up_dot = jnp.zeros((1, step), f32)
        for j in range(TOKENS):
            gate_dot = jnp.where(token == j, dots[j : j + 1], gate_dot)
            up_dot = jnp.where(token == j, dots[TOKENS + j : TOKENS + j + 1], up_dot)
        gate_pre = picked[:OWN] + spread * gate_dot * right[:OWN]
        up_pre = picked[OWN:] + spread * up_dot * right[OWN:]
        out_ref[:, rows] = (gate_pre / (1.0 + jnp.exp(-gate_pre)) * up_pre).astype(bf16)


def activate(ids, base, dots, rights):
    return pl.pallas_call(
        hidden_kernel,
        out_shape=jax.ShapeDtypeStruct((OWN, ROWS), bf16),
        compiler_params=pltpu.CompilerParams(vmem_limit_bytes=32 * 1024 * 1024),
    )(ids, base, dots, rights)


def outer_sum(left, right):
    high = lax.reduce_precision(left, 8, 7)
    low = left - high
    dims = (((0,), (0,)), ((), ()))
    return lax.dot_general(
        high.astype(bf16), right, dims, preferred_element_type=f32
    ) + lax.dot_general(low.astype(bf16), right, dims, preferred_element_type=f32)


def outer_sum_right(left, right):
    high = lax.reduce_precision(right, 8, 7)
    low = right - high
    dims = (((0,), (0,)), ((), ()))
    return lax.dot_general(
        left, high.astype(bf16), dims, preferred_element_type=f32
    ) + lax.dot_general(left, low.astype(bf16), dims, preferred_element_type=f32)


def per_device(
    states,
    token_ids,
    gate_matrix,
    up_matrix,
    down_matrix,
    gate_left,
    gate_right,
    up_left,
    up_right,
    down_left,
    down_right,
    target,
):
    x_index = lax.axis_index("x")
    tp_index = lax.axis_index(TP)

    down_all = lax.all_gather(down_matrix, "x", axis=0, tiled=True)
    left_down = lax.all_gather(
        down_left.reshape(GROUP * 4, UNITS // 4), POP, axis=0, tiled=True
    ).reshape(MEMBERS, UNITS)
    rights = lax.all_gather(
        jnp.concatenate([gate_right, up_right], axis=0), POP, axis=0, tiled=True
    ).reshape(NX * NYH, 2, GROUP, UNITS)
    right_gate = rights[:, 0].reshape(MEMBERS, UNITS)
    right_up = rights[:, 1].reshape(MEMBERS, UNITS)
    own_right = lax.dynamic_slice_in_dim(down_right, tp_index * BLOCK_MEMBERS, BLOCK_MEMBERS, 0)
    forth = to_owner()
    back = [(b, a) for a, b in forth]
    moved = lax.ppermute(jnp.concatenate([target, own_right], axis=0), EVERY, back)
    piece_target, piece_right = moved[:BLOCK].astype(f32), moved[BLOCK:].astype(f32)

    dims = (((0,), (1,)), ((), ()))
    gate_part = lax.dot_general(gate_matrix, states, dims, preferred_element_type=f32)
    up_part = lax.dot_general(up_matrix, states, dims, preferred_element_type=f32)
    ids = token_ids.T
    bank = lax.broadcasted_iota(jnp.int32, (BANK, MEMBERS), 0)
    dots = []
    for left in (gate_left, up_left):
        inner = lax.dot_general(states, left, (((1,), (1,)), ((), ())), preferred_element_type=f32)
        for j in range(TOKENS):
            dots.append(jnp.sum(jnp.where(bank == ids[j : j + 1], inner, 0.0), axis=0))
    dots = jnp.pad(jnp.stack(dots), ((0, 0), (0, 3 * BANK - MEMBERS)))
    dots = dots.reshape(8, 3, BANK).transpose(1, 0, 2).reshape(24, BANK)

    first = jnp.concatenate(
        [
            gate_part.reshape(NX, 128, BANK),
            up_part.reshape(NX, 128, BANK),
            jnp.broadcast_to(dots, (NX, 24, BANK)),
            jnp.concatenate(
                [
                    gate_right.astype(f32).reshape(GROUP, NX, 128),
                    up_right.astype(f32).reshape(GROUP, NX, 128),
                ],
                axis=2,
            ).transpose(1, 0, 2),
        ],
        axis=1,
    )
    first = lax.all_to_all(first, "x", 0, 0)
    summed = jnp.sum(first[:, :280], axis=0)
    factors = first[:, 280:].reshape(X_MEMBERS, 2, NYH, OWN)
    factors = factors.transpose(2, 1, 3, 0).reshape(NYH, 2 * OWN, X_MEMBERS)
    second = jnp.concatenate(
        [
            summed[:256]
            .reshape(2, NYH, OWN, BANK)
            .transpose(1, 0, 2, 3)
            .reshape(NYH, 2 * OWN, BANK),
            jnp.broadcast_to(summed[256:], (NYH, 24, BANK)),
            jnp.pad(factors, ((0, 0), (0, 0), (0, BANK - X_MEMBERS))),
        ],
        axis=1,
    )
    second = lax.all_to_all(second, "yh", 0, 0)
    summed = jnp.sum(second[:, :88], axis=0)
    base = summed[:64]
    dots = summed[64:].reshape(3, 8, BANK).transpose(1, 0, 2).reshape(8, 3 * BANK)[:, :MEMBERS]
    factors = second[:, 88:, :X_MEMBERS].astype(bf16).reshape(NYH, 2 * OWN, NX, GROUP)
    factors = factors.transpose(1, 2, 0, 3).reshape(2 * OWN, MEMBERS)
    own_hidden = activate(token_ids.reshape(1, ROWS), base, dots, factors)

    outgoing = jnp.broadcast_to(
        own_hidden.reshape(OWN, NX, X_ROWS).transpose(1, 0, 2)[:, None],
        (NX, NYH, OWN, X_ROWS),
    ).reshape(NX * NYH * OWN, X_ROWS)
    hidden = lax.all_to_all(outgoing, POP, 0, 0, tiled=True)

    x_left = lax.dynamic_slice_in_dim(left_down, x_index * X_MEMBERS, X_MEMBERS, 0)
    against = lax.dot_general(hidden, x_left, (((0,), (1,)), ((), ())), preferred_element_type=f32)
    own_member = (
        lax.broadcasted_iota(jnp.int32, (X_ROWS, X_MEMBERS), 0) // TOKENS
        == lax.broadcasted_iota(jnp.int32, (X_ROWS, X_MEMBERS), 1)
    )
    down_dots = jnp.sum(jnp.where(own_member, against, 0.0), axis=1, keepdims=True)
    at_dot = lax.broadcasted_iota(jnp.int32, (X_ROWS, PADDED), 1) == WIDTH
    slices = []
    for x in range(NX):
        part = lax.dot_general(
            hidden,
            down_all[x * UNITS : (x + 1) * UNITS],
            (((0,), (0,)), ((), ())),
            preferred_element_type=f32,
        )
        part = jnp.pad(part, ((0, 0), (0, PADDED - WIDTH)))
        slices.append(jnp.where(at_dot, down_dots, part))
    sent = jnp.stack([jnp.stack([slices[0], slices[2]]), jnp.stack([slices[1], slices[3]])])
    got = lax.all_to_all(sent, "c", 0, 0)
    pair = (got[0] + got[1]).astype(bf16)
    pair = pair.reshape(NYL, NZ, BLOCK, PADDED).transpose(1, 0, 2, 3)
    got = lax.all_to_all(pair.reshape(NZ * NYL, BLOCK, PADDED), ("z", "yl"), 0, 0)
    total = jnp.sum(got.astype(f32), axis=0)
    scaled_dot = spread * (total[:, WIDTH : WIDTH + 1] * (1.0 / math.sqrt(FF)))
    extra = scaled_dot.reshape(BLOCK_MEMBERS, TOKENS, 1) * piece_right[:, None, :]
    raw = total[:, :WIDTH] + extra.reshape(BLOCK, WIDTH)
    raw_out = lax.ppermute(raw, EVERY, forth)

    error = raw - piece_target
    part_loss = jnp.sum((error * error).reshape(BLOCK_MEMBERS, TOKENS * WIDTH), axis=1)
    lanes = jnp.pad(part_loss[None, :], ((0, 7), (0, 128 - BLOCK_MEMBERS)))
    near = lax.all_to_all(
        jnp.broadcast_to(lanes, (NYH * NYL * NC, 8, 128)), ("yh", "yl", "c"), 0, 0
    )
    block_loss = jnp.sum(near, axis=0)
    far = lax.all_to_all(jnp.broadcast_to(block_loss, (NX * NZ, 8, 128)), ("x", "z"), 0, 0)
    losses = far[:, 0, :BLOCK_MEMBERS].reshape(MEMBERS) / (TOKENS * D)

    mean_loss = jnp.mean(losses)
    spread_loss = jnp.mean((losses - mean_loss) ** 2)
    weights = -(losses - mean_loss) / jnp.sqrt(spread_loss + epsilon) * (1.0 / math.sqrt(MEMBERS))
    gate_update = outer_sum(weights[:, None] * gate_left.astype(f32), right_gate)
    up_update = outer_sum(weights[:, None] * up_left.astype(f32), right_up)
    down_update = outer_sum_right(left_down, weights[:, None] * down_right.astype(f32))
    return (raw_out, gate_update, up_update, down_update)


def solution(mesh):
    cut = Mesh(mesh.devices.reshape(NX, NYH, NZ, NYL, NC), EVERY)
    return jax.shard_map(
        per_device,
        mesh=cut,
        in_specs=(
            P(None, POP),
            P(),
            P(POP, TP),
            P(POP, TP),
            P(TP, POP),
            P(None, POP),
            P(POP, TP),
            P(None, POP),
            P(POP, TP),
            P(POP, TP),
            P(None, POP),
            P(TP, POP),
        ),
        out_specs=(P(TP, POP), P(POP, TP), P(POP, TP), P(TP, POP)),
        check_vma=False,
    )
```

```python
import math

import jax
import jax.numpy as jnp
from jax import lax
from jax.experimental import pallas as pl
from jax.experimental.pallas import tpu as pltpu
from jax.sharding import Mesh, PartitionSpec as P

D = 5120
FF = 16384
MEMBERS = 640
TOKENS = 4
ROWS = MEMBERS * TOKENS
BANK = 256

spread = 0.5
epsilon = 1e-06

f32 = jnp.float32
bf16 = jnp.bfloat16

NX, NYH, NZH, NZL, NYL, NC = 4, 4, 4, 2, 2, 2
POP = ("x", "yh")
TP = ("zh", "zl", "yl", "c")
EVERY = POP + TP
GROUP = MEMBERS // (NX * NYH)
UNITS = 512
OWN = UNITS // (NX * NYH)
WIDTH = D // (NX * NYH)
CHUNK = 128
CHUNKS = MEMBERS // CHUNK
PART = ROWS // (NX * NC)
BLOCK = ROWS // (NZH * NZL * NYL * NC)
BLOCK_MEMBERS = BLOCK // TOKENS
PADDED = 384
REST = PADDED - PART
KEPT = UNITS + CHUNK


def to_owner():
    pairs = []
    for x in range(NX):
        for yh in range(NYH):
            for zh in range(NZH):
                for column in range(NZL * NYL):
                    for c in range(NC):
                        here = (x * NYH + yh) * 32 + (zh * 4 + column) * NC + c
                        row = (zh * NX + x) * NC + c
                        pairs.append((here, (column * NYH + yh) * 32 + row))
    return pairs


def split_three(value):
    high = value.astype(bf16)
    rest = value - high.astype(f32)
    middle = rest.astype(bf16)
    low = (rest - middle.astype(f32)).astype(bf16)
    return high, middle, low


SMEM = pl.BlockSpec(memory_space=pltpu.SMEM)
VMEM = pl.BlockSpec(memory_space=pltpu.VMEM)
ANY = pl.BlockSpec(memory_space=pl.ANY)
PARAMS = pltpu.CompilerParams(vmem_limit_bytes=40 * 1024 * 1024)
WIDE = pltpu.CompilerParams(vmem_limit_bytes=60 * 1024 * 1024)
NT = (((1,), (1,)), ((), ()))


def fetch(sources, targets, arrived):
    copies = [
        pltpu.make_async_copy(source, target, arrived.at[k])
        for k, (source, target) in enumerate(zip(sources, targets, strict=True))
    ]
    for copy in copies:
        copy.start()
    return copies


def front_kernel(*refs):
    out_ref, held, arrived = refs[9], refs[10:19], refs[19]
    copies = fetch(refs[:9], held, arrived)
    ids_ref, states_ref, gate_left_ref, up_left_ref, gate_ref, up_ref = held[:6]
    copies[0].wait()
    copies[1].wait()
    states = jnp.transpose(states_ref[...].astype(f32)).astype(bf16)
    bank = lax.broadcasted_iota(jnp.int32, (BANK, MEMBERS), 0)
    line = lax.broadcasted_iota(jnp.int32, (8, MEMBERS), 0)
    dots = jnp.zeros((8, MEMBERS), f32)
    for kind, left in enumerate((gate_left_ref, up_left_ref)):
        copies[2 + kind].wait()
        inner = jnp.dot(states, left[...], preferred_element_type=f32)
        for j in range(TOKENS):
            chosen = jnp.where(bank == ids_ref[j : j + 1, :], inner, 0.0)
            row = jnp.sum(chosen, axis=0, keepdims=True)
            dots = jnp.where(line == kind * TOKENS + j, row, dots)
    groups = [x * NYH + yh for yh in range(NYH) for x in range(NX)]
    dots = jnp.concatenate([dots[:, g * GROUP : (g + 1) * GROUP] for g in groups], axis=1)
    for kind, matrix in enumerate((gate_ref, up_ref)):
        copies[4 + kind].wait()
        part = jnp.dot(states, matrix[...], preferred_element_type=f32)
        for x in range(NX):
            out_ref[x, kind * BANK : (kind + 1) * BANK] = part[:, x * CHUNK : (x + 1) * CHUNK]
    for kind in range(3):
        copies[6 + kind].wait()
        start = 2 * BANK + kind * GROUP
        for x in range(NX):
            out_ref[x, start : start + GROUP] = held[6 + kind][
                :, x * CHUNK : (x + 1) * CHUNK
            ].astype(f32)
    for x in range(NX):
        for k in range(CHUNKS):
            start = 2 * BANK + 3 * GROUP + 8 * k
            out_ref[x, start : start + 8] = dots[:, k * CHUNK : (k + 1) * CHUNK]


def front(*arrays):
    return pl.pallas_call(
        front_kernel,
        out_shape=jax.ShapeDtypeStruct((NX, 2 * BANK + 4 * GROUP, CHUNK), f32),
        in_specs=[ANY] * 9,
        scratch_shapes=[pltpu.VMEM(array.shape, array.dtype) for array in arrays]
        + [pltpu.SemaphoreType.DMA((9,))],
        compiler_params=WIDE,
    )(*arrays)


def middle_kernel(got_ref, out_ref):
    base = got_ref[0, : 2 * BANK]
    dots = got_ref[0, 2 * BANK + 3 * GROUP :]
    for x in range(1, NX):
        base += got_ref[x, : 2 * BANK]
        dots += got_ref[x, 2 * BANK + 3 * GROUP :]
    base = jnp.transpose(base)
    rights = []
    for kind in range(3):
        start = 2 * BANK + kind * GROUP
        rights += [got_ref[x, start : start + GROUP] for x in range(NX)]
    rights.append(jnp.zeros((2 * BANK - 3 * NX * GROUP, CHUNK), f32))
    rights = jnp.transpose(jnp.concatenate(rights, axis=0))
    for yh in range(NYH):
        out_ref[yh, :OWN] = base[yh * OWN : (yh + 1) * OWN]
        out_ref[yh, OWN : 2 * OWN] = rights[yh * OWN : (yh + 1) * OWN]
        out_ref[yh, 2 * OWN + 8 :] = jnp.zeros((8, 2 * BANK), f32)
        for k in range(CHUNKS):
            line = 2 * OWN + 8 * (k // 4)
            lane = (k % 4) * CHUNK
            out_ref[yh, line : line + 8, lane : lane + CHUNK] = dots[8 * k : 8 * k + 8]


def middle(got):
    return pl.pallas_call(
        middle_kernel,
        out_shape=jax.ShapeDtypeStruct((NYH, 2 * OWN + 16, 2 * BANK), f32),
        compiler_params=PARAMS,
    )(got)


def columns_kernel(place_ref, down_ref, right_ref, *out_refs):
    member = lax.broadcasted_iota(jnp.int32, (MEMBERS, CHUNK), 0)
    lane = lax.broadcasted_iota(jnp.int32, (MEMBERS, CHUNK), 1)
    quarter = BLOCK_MEMBERS
    row = sum((lane >= k * quarter).astype(jnp.int32) for k in range(1, NZH))
    wanted = lane + row * (NX * NC - 1) * quarter
    right = right_ref[...]
    for out_ref in out_refs:
        out_ref[:, :UNITS] = down_ref[...]
    for k in range(NX):
        start = (lax.rem(place_ref[0] + k, NX) * NC + place_ref[2]) * quarter
        chosen = member == jnp.where(lane < NZH * quarter, wanted + start, MEMBERS)
        chosen = jnp.dot(
            right, chosen.astype(f32).astype(bf16), preferred_element_type=f32
        ).astype(bf16)
        if k == 2:
            for out_ref in out_refs[1:]:
                out_ref[:, KEPT:] = chosen
        else:
            out_refs[(0, 1, None, 2)[k]][:, UNITS:KEPT] = chosen


def down_columns(place, down, right):
    own = jax.ShapeDtypeStruct((WIDTH, KEPT), bf16)
    leaving = jax.ShapeDtypeStruct((WIDTH, KEPT + CHUNK), bf16)
    return pl.pallas_call(
        columns_kernel,
        out_shape=[own, leaving, leaving],
        in_specs=[SMEM, VMEM, VMEM],
        compiler_params=PARAMS,
    )(place, down, right)


def hidden_kernel(ids_ref, got_ref, out_ref, hidden_ref, down_ref):
    base = got_ref[0, :OWN]
    all_dots = got_ref[0, 2 * OWN :]
    for yh in range(1, NYH):
        base += got_ref[yh, :OWN]
        all_dots += got_ref[yh, 2 * OWN :]
    along = NX * GROUP
    rights = [
        jnp.concatenate(
            [
                got_ref[yh, OWN : 2 * OWN, kind * along : (kind + 1) * along]
                for yh in range(NYH)
            ],
            axis=1,
        )
        for kind in range(3)
    ]
    rights = jnp.concatenate(rights, axis=0).astype(bf16)
    step = CHUNK * TOKENS
    scale = f32(1.0 / math.sqrt(D))
    base = jnp.concatenate([base[:, :BANK], base[:, BANK:]], axis=0)
    base = jnp.concatenate(split_three(base), axis=0)
    repeat = (
        lax.broadcasted_iota(jnp.int32, (CHUNK, step), 1) // TOKENS
        == lax.broadcasted_iota(jnp.int32, (CHUNK, step), 0)
    ).astype(f32).astype(bf16)
    token = lax.broadcasted_iota(jnp.int32, (1, step), 1) % TOKENS
    for part in range(CHUNKS):
        rows = slice(part * step, (part + 1) * step)
        chosen = (
            lax.broadcasted_iota(jnp.int32, (BANK, step), 0) == ids_ref[:, rows]
        ).astype(f32).astype(bf16)
        picked = jnp.dot(base, chosen, preferred_element_type=f32)
        picked = picked[: 2 * OWN] + picked[2 * OWN : 4 * OWN] + picked[4 * OWN :]
        line, lane = 8 * (part // 4), (part % 4) * CHUNK
        dots = all_dots[line : line + 8, lane : lane + CHUNK]
        dots = jnp.concatenate(split_three(dots), axis=0)
        dots = jnp.dot(dots, repeat, preferred_element_type=f32)
        dots = (dots[:8] + dots[8:16] + dots[16:]) * scale
        right = jnp.dot(
            rights[:, part * CHUNK : (part + 1) * CHUNK], repeat, preferred_element_type=f32
        )
        gate_dot = jnp.zeros((1, step), f32)
        up_dot = jnp.zeros((1, step), f32)
        for j in range(TOKENS):
            gate_dot = jnp.where(token == j, dots[j : j + 1], gate_dot)
            up_dot = jnp.where(token == j, dots[TOKENS + j : TOKENS + j + 1], up_dot)
        gate_pre = picked[:OWN] + spread * gate_dot * right[:OWN]
        up_pre = picked[OWN:] + spread * up_dot * right[OWN : 2 * OWN]
        hidden = (gate_pre / (1.0 + jnp.exp(-gate_pre)) * up_pre).astype(bf16)
        hidden_ref[:, rows] = hidden
        down_ref[:, rows] = jnp.sum(
            hidden.astype(f32) * right[2 * OWN :], axis=0, keepdims=True
        )
    line = lax.broadcasted_iota(jnp.int32, (OWN, REST), 0)
    for x in range(NX):
        for c in range(NC):
            starts = [((x * NZH + zh) * NC + c) * BLOCK for zh in range(NZH)]
            dots = jnp.concatenate([down_ref[:, k : k + BLOCK] for k in starts], axis=1)
            down = jnp.zeros((OWN, REST), f32)
            for k in range(PART // REST):
                piece = dots[:, k * REST : (k + 1) * REST]
                high = piece.astype(bf16).astype(f32)
                down = jnp.where(line == k, high, down)
                down = jnp.where(line == k + 8, piece - high, down)
            block = jnp.concatenate(
                [hidden_ref[:, k : k + BLOCK].astype(f32) for k in starts] + [down], axis=1
            ).astype(bf16)
            for yh in range(NYH):
                out_ref[c, x, yh] = block


def activate(ids, got):
    return pl.pallas_call(
        hidden_kernel,
        out_shape=jax.ShapeDtypeStruct((NC, NX, NYH, OWN, PADDED), bf16),
        scratch_shapes=[pltpu.VMEM((OWN, ROWS), bf16), pltpu.VMEM((1, ROWS), f32)],
        compiler_params=PARAMS,
    )(ids, got)


def project_kernel(place_ref, hidden_ref, *refs):
    out_ref, held, arrived = refs[2 * NX], refs[2 * NX + 1 : 4 * NX + 1], refs[4 * NX + 1]
    own = list(refs[:NX])
    own[1], own[3] = own[1].at[:, :KEPT], own[3].at[:, :KEPT]
    other = [ref.at[:, :UNITS] for ref in refs[NX : 2 * NX]]
    copies = fetch(own + other, held, arrived)
    own_refs, other_refs = held[:NX], held[NX:]
    x_here, c_here = place_ref[0], place_ref[2]
    dots = jnp.zeros((16, CHUNK), f32)
    for source in range(NC * NX * NYH):
        dots += hidden_ref[source * OWN : source * OWN + 16, PADDED - CHUNK :].astype(f32)
    dots = dots[:8] + dots[8:]
    eye = lax.broadcasted_iota(jnp.int32, (REST, REST), 0) == lax.broadcasted_iota(
        jnp.int32, (REST, REST), 1
    )
    columns = []
    for k in range(PART // REST):
        row = dots[k : k + 1, CHUNK - REST :]
        columns.append(jnp.sum(jnp.where(eye, row, 0.0), axis=1, keepdims=True))
    dot = jnp.concatenate(columns, axis=0) * f32(spread / math.sqrt(FF))
    own_member = (
        lax.broadcasted_iota(jnp.int32, (PART, CHUNK), 0) // TOKENS
        == lax.broadcasted_iota(jnp.int32, (PART, CHUNK), 1)
    )
    shares = jnp.where(own_member, dot, 0.0)
    high = shares.astype(bf16)
    low = (shares - high.astype(f32)).astype(bf16)
    shares = jnp.concatenate([high, low], axis=1)
    start = pl.multiple_of(c_here * UNITS, UNITS)
    own_rows = hidden_ref[pl.ds(start, UNITS), :].astype(f32)
    start = pl.multiple_of((1 - c_here) * UNITS, UNITS)
    other_rows = hidden_ref[pl.ds(start, UNITS), :].astype(f32)
    own_rows = jnp.transpose(own_rows)[:PART].astype(bf16)
    other_rows = jnp.transpose(other_rows)[:PART].astype(bf16)
    for k in range(NX):
        x = lax.rem(x_here - k + NX, NX)
        copies[k].wait()
        copies[NX + k].wait()
        total = lax.dot_general(
            own_rows, own_refs[k][:, :UNITS], NT, preferred_element_type=f32
        )
        total += lax.dot_general(
            other_rows, other_refs[k][...], NT, preferred_element_type=f32
        )
        right = own_refs[k][:, KEPT:] if k == 2 else own_refs[k][:, UNITS:KEPT]
        right = jnp.concatenate([right, right], axis=1)
        total += lax.dot_general(shares, right, NT, preferred_element_type=f32)
        for zh in range(NZH):
            top = total[zh * BLOCK : zh * BLOCK + BLOCK // 2]
            bottom = total[zh * BLOCK + BLOCK // 2 : (zh + 1) * BLOCK]
            out_ref[zh * NX + x] = jnp.concatenate([top, bottom], axis=1).astype(bf16)


def project(place, hidden, own, other):
    return pl.pallas_call(
        project_kernel,
        out_shape=jax.ShapeDtypeStruct((NZH * NX, BLOCK // 2, 2 * WIDTH), bf16),
        in_specs=[SMEM, VMEM] + [ANY] * (2 * NX),
        scratch_shapes=[
            pltpu.VMEM((WIDTH, KEPT + CHUNK if k == 2 else KEPT), bf16) for k in range(NX)
        ]
        + [pltpu.VMEM((WIDTH, UNITS), bf16)] * NX
        + [pltpu.SemaphoreType.DMA((2 * NX,))],
        compiler_params=WIDE,
    )(place, hidden, *own, *other)


def loss_kernel(place_ref, got_ref, target_ref, raw_ref, out_ref):
    total = got_ref[0].astype(f32)
    for source in range(1, NZH * NX):
        total += got_ref[source].astype(f32)
    raw = jnp.concatenate([total[:, :WIDTH], total[:, WIDTH:]], axis=0)
    raw_ref[...] = raw
    error = raw - target_ref[...].astype(f32)
    squares = jnp.sum(error * error, axis=1, keepdims=True)
    member = (
        lax.broadcasted_iota(jnp.int32, (BLOCK, CHUNK), 0) // TOKENS
        + place_ref[3] * BLOCK_MEMBERS
        - lax.broadcasted_iota(jnp.int32, (BLOCK, CHUNK), 1)
    )
    line = lax.broadcasted_iota(jnp.int32, (8, CHUNK), 0)
    placed = jnp.zeros((8, CHUNK), f32)
    for k in range(CHUNKS):
        here = jnp.sum(jnp.where(member == k * CHUNK, squares, 0.0), axis=0, keepdims=True)
        placed = jnp.where(line == k, here, placed)
    for k in range(NYH * NZL * NYL):
        out_ref[k] = placed


def piece_losses(place, got, target):
    return pl.pallas_call(
        loss_kernel,
        out_shape=[
            jax.ShapeDtypeStruct((BLOCK, WIDTH), f32),
            jax.ShapeDtypeStruct((NYH * NZL * NYL, 8, CHUNK), f32),
        ],
        in_specs=[SMEM] + [VMEM] * 2,
        compiler_params=PARAMS,
    )(place, got, target)


def update_kernel(place_ref, far_ref, *refs):
    left_hbm, blocks = refs[:3], refs[3:7]
    out_hbm, factor_ref, left_refs = refs[7:10], refs[10], refs[11:14]
    out_refs, arrived, left_sem = refs[14:17], refs[17], refs[18]
    copies = fetch(left_hbm, left_refs, arrived)
    leaving = []
    x_here = place_ref[0]
    group = NYH * GROUP
    for kind in range(3):
        for k, block in enumerate(blocks):
            start = pl.multiple_of(lax.rem(x_here - k + NX, NX) * group, group)
            factor_ref[kind, pl.ds(start, group), :] = block[kind]
    losses = far_ref[0]
    for source in range(1, NX * NC * NZH):
        losses += far_ref[source]
    losses = losses * f32(1.0 / (TOKENS * D))
    valid = lax.broadcasted_iota(jnp.int32, (8, CHUNK), 0) < CHUNKS
    mean = jnp.sum(losses, keepdims=True) * f32(1.0 / MEMBERS)
    offset = jnp.where(valid, losses - mean, 0.0)
    variance = jnp.sum(offset * offset, keepdims=True) * f32(1.0 / MEMBERS)
    weights = -offset / jnp.sqrt(variance + epsilon) * f32(1.0 / math.sqrt(MEMBERS))
    weights = jnp.concatenate([weights[k : k + 1] for k in range(CHUNKS)], axis=1)
    for kind in range(3):
        copies[kind].wait()
        scaled = left_refs[kind][...].astype(f32) * weights
        high = scaled.astype(bf16)
        low = (scaled - high.astype(f32)).astype(bf16)
        for part in range(2):
            lines = slice(part * (WIDTH // 2), (part + 1) * (WIDTH // 2))
            out_refs[kind][lines] = jnp.dot(
                high[lines], factor_ref[kind], preferred_element_type=f32
            ) + jnp.dot(low[lines], factor_ref[kind], preferred_element_type=f32)
            copy = pltpu.make_async_copy(
                out_refs[kind].at[lines], out_hbm[kind].at[lines], left_sem.at[2 * kind + part]
            )
            copy.start()
            leaving.append(copy)
    for copy in leaving:
        copy.wait()


def updates(place, far, lefts, blocks):
    out = jax.ShapeDtypeStruct((WIDTH, UNITS), f32)
    return pl.pallas_call(
        update_kernel,
        out_shape=[out] * 3,
        in_specs=[SMEM, VMEM] + [ANY] * 3 + [VMEM] * NX,
        out_specs=[ANY] * 3,
        scratch_shapes=[pltpu.VMEM((3, MEMBERS, UNITS), bf16)]
        + [pltpu.VMEM((WIDTH, MEMBERS), bf16)] * 3
        + [pltpu.VMEM((WIDTH, UNITS), f32)] * 3
        + [pltpu.SemaphoreType.DMA((3,)), pltpu.SemaphoreType.DMA((6,))],
        compiler_params=WIDE,
    )(place, far, *lefts, *blocks)


def after(earlier, *arrays):
    return lax.optimization_barrier((earlier, *arrays))[1:]


def shifted(value, axis, size, k):
    return lax.ppermute(value, axis, [(i, (i + k) % size) for i in range(size)])


def per_device(
    states,
    token_ids,
    gate_matrix,
    up_matrix,
    down_matrix,
    gate_left,
    gate_right,
    up_left,
    up_right,
    down_left,
    down_right,
    target,
):
    x_index, yh_index, c_index = (lax.axis_index(axis) for axis in ("x", "yh", "c"))
    block = (lax.axis_index("zh") * NX + x_index) * NC + c_index
    place = jnp.stack([x_index, yh_index, c_index, block]).astype(jnp.int32)
    forth = to_owner()
    back = [(b, a) for a, b in forth]

    own_factors = jnp.concatenate([gate_right, up_right, down_left], axis=0)
    along = [shifted(own_factors, "yh", NYH, k) for k in (1, 2, 3)]
    columns = down_columns(place, down_matrix.T, down_right.T)

    got = front(
        token_ids.T,
        states.T,
        gate_left.T,
        up_left.T,
        gate_matrix,
        up_matrix,
        gate_right,
        up_right,
        down_left,
    )
    sent = middle(lax.all_to_all(got, "x", 0, 0))
    piece_target = lax.ppermute(target, EVERY, back)
    partner = shifted(columns[0], "c", NC, 1)
    sent, along[0], along[2], columns, piece_target, partner = lax.optimization_barrier(
        (sent, along[0], along[2], columns, piece_target, partner)
    )
    got = lax.all_to_all(sent, "yh", 0, 0)

    before = shifted(columns[1], "x", NX, 1)
    later = shifted(columns[2], "x", NX, 3)
    ids = token_ids.reshape(NX, NYH, GROUP * TOKENS).transpose(1, 0, 2).reshape(1, ROWS)
    outgoing = activate(ids, got)
    outgoing, before, later, along[1] = lax.optimization_barrier(
        (outgoing, before, later, along[1])
    )

    hidden = lax.all_to_all(
        outgoing.reshape(NC * NX * NYH * OWN, PADDED), ("c", "x", "yh"), 0, 0, tiled=True
    )
    half = WIDTH // 2
    opposite = jnp.concatenate(
        [shifted(before[:half], "x", NX, 1), shifted(later[half:], "x", NX, 3)], axis=0
    )
    columns = [columns[0], before, opposite, later]
    others = [partner] + [shifted(column, "c", NC, 1) for column in columns[1:]]

    pieces = project(place, hidden, columns, others)
    (along,) = after(hidden, along)
    got = lax.all_to_all(pieces, ("zh", "zl", "yl"), 0, 0)
    around = jnp.stack([own_factors] + along).reshape(NYH, 3, GROUP, UNITS)
    around = jnp.concatenate(
        [
            lax.dynamic_index_in_dim(around, lax.rem(yh_index - k + NYH, NYH), 0, keepdims=False)
            for k in range(NYH)
        ],
        axis=1,
    )
    arounds = [shifted(around, "x", NX, k) for k in (1, 2, 3)]
    raw, sent = piece_losses(place, got, piece_target)
    raw_out = lax.ppermute(raw, EVERY, forth)

    near = lax.all_to_all(sent, ("yh", "zl", "yl"), 0, 0)
    near = jnp.broadcast_to(jnp.sum(near, axis=0), (NX * NC * NZH, 8, CHUNK))
    near, arounds = lax.optimization_barrier((near, arounds))
    far = lax.all_to_all(near, ("x", "c", "zh"), 0, 0)
    gate_update, up_update, down_update = updates(
        place,
        far,
        (gate_left.T, up_left.T, down_right.T),
        (around, *arounds),
    )
    return (raw_out, gate_update, up_update, down_update.T)


def solution(mesh):
    cut = Mesh(mesh.devices.reshape(NX, NYH, NZH, NZL, NYL, NC), EVERY)
    return jax.shard_map(
        per_device,
        mesh=cut,
        in_specs=(
            P(None, POP),
            P(),
            P(POP, TP),
            P(POP, TP),
            P(TP, POP),
            P(None, POP),
            P(POP, TP),
            P(None, POP),
            P(POP, TP),
            P(POP, TP),
            P(None, POP),
            P(TP, POP),
        ),
        out_specs=(P(TP, POP), P(POP, TP), P(POP, TP), P(TP, POP)),
        check_vma=False,
    )
```

```python
import math

import jax
import jax.numpy as jnp
from jax import lax
from jax.experimental import pallas as pl
from jax.experimental.pallas import tpu as pltpu
from jax.sharding import Mesh, PartitionSpec as P

D = 5120
FF = 16384
MEMBERS = 640
TOKENS = 4
ROWS = MEMBERS * TOKENS
BANK = 256

spread = 0.5
epsilon = 1e-06

f32 = jnp.float32
bf16 = jnp.bfloat16

NX, NYH, NZH, NZL, NYL, NC = 4, 4, 4, 2, 2, 2
POP = ("x", "yh")
TP = ("zh", "zl", "yl", "c")
EVERY = POP + TP
GROUP = MEMBERS // (NX * NYH)
UNITS = 512
OWN = UNITS // (NX * NYH)
WIDTH = D // (NX * NYH)
CHUNK = 128
CHUNKS = MEMBERS // CHUNK
PART = ROWS // (NX * NC)
BLOCK = ROWS // (NZH * NZL * NYL * NC)
BLOCK_MEMBERS = BLOCK // TOKENS
PADDED = 384
REST = PADDED - PART
KEPT = UNITS + CHUNK


def to_owner():
    pairs = []
    for x in range(NX):
        for yh in range(NYH):
            for zh in range(NZH):
                for column in range(NZL * NYL):
                    for c in range(NC):
                        here = (x * NYH + yh) * 32 + (zh * 4 + column) * NC + c
                        row = (zh * NX + x) * NC + c
                        pairs.append((here, (column * NYH + yh) * 32 + row))
    return pairs


def split_three(value):
    high = value.astype(bf16)
    rest = value - high.astype(f32)
    middle = rest.astype(bf16)
    low = (rest - middle.astype(f32)).astype(bf16)
    return high, middle, low


SMEM = pl.BlockSpec(memory_space=pltpu.SMEM)
VMEM = pl.BlockSpec(memory_space=pltpu.VMEM)
WIDE = pltpu.CompilerParams(vmem_limit_bytes=60 * 1024 * 1024)
HBM = pl.BlockSpec(memory_space=pltpu.HBM)
PARAMS = pltpu.CompilerParams(vmem_limit_bytes=24 * 1024 * 1024)
NT = (((1,), (1,)), ((), ()))


def fetch(sources, targets, arrived):
    copies = [
        pltpu.make_async_copy(source, target, arrived.at[k])
        for k, (source, target) in enumerate(zip(sources, targets, strict=True))
    ]
    for copy in copies:
        copy.start()
    return copies


def front_kernel(*refs):
    out_ref, factors_ref, held, arrived = refs[9], refs[10], refs[11:20], refs[20]
    copies = fetch(refs[:9], held, arrived)
    ids_ref, states_ref, gate_left_ref, up_left_ref, gate_ref, up_ref = held[:6]
    copies[0].wait()
    copies[1].wait()
    states = jnp.transpose(states_ref[...].astype(f32)).astype(bf16)
    bank = lax.broadcasted_iota(jnp.int32, (BANK, MEMBERS), 0)
    line = lax.broadcasted_iota(jnp.int32, (8, MEMBERS), 0)
    dots = jnp.zeros((8, MEMBERS), f32)
    for kind, left in enumerate((gate_left_ref, up_left_ref)):
        copies[2 + kind].wait()
        inner = jnp.dot(states, left[...], preferred_element_type=f32)
        for j in range(TOKENS):
            chosen = jnp.where(bank == ids_ref[j : j + 1, :], inner, 0.0)
            row = jnp.sum(chosen, axis=0, keepdims=True)
            dots = jnp.where(line == kind * TOKENS + j, row, dots)
    groups = [x * NYH + yh for yh in range(NYH) for x in range(NX)]
    dots = jnp.concatenate([dots[:, g * GROUP : (g + 1) * GROUP] for g in groups], axis=1)
    for kind, matrix in enumerate((gate_ref, up_ref)):
        copies[4 + kind].wait()
        part = jnp.dot(states, matrix[...], preferred_element_type=f32)
        for x in range(NX):
            out_ref[x, kind * BANK : (kind + 1) * BANK] = part[:, x * CHUNK : (x + 1) * CHUNK]
    for kind in range(3):
        copies[6 + kind].wait()
        factors_ref[kind * GROUP : (kind + 1) * GROUP] = held[6 + kind][...]
        start = 2 * BANK + kind * GROUP
        for x in range(NX):
            out_ref[x, start : start + GROUP] = held[6 + kind][
                :, x * CHUNK : (x + 1) * CHUNK
            ].astype(f32)
    for x in range(NX):
        for k in range(CHUNKS):
            start = 2 * BANK + 3 * GROUP + 8 * k
            out_ref[x, start : start + 8] = dots[:, k * CHUNK : (k + 1) * CHUNK]


def front(*arrays):
    return pl.pallas_call(
        front_kernel,
        out_shape=[
            jax.ShapeDtypeStruct((NX, 2 * BANK + 4 * GROUP, CHUNK), f32),
            jax.ShapeDtypeStruct((3 * GROUP, UNITS), bf16),
        ],
        in_specs=[HBM] * 9,
        scratch_shapes=[pltpu.VMEM(array.shape, array.dtype) for array in arrays]
        + [pltpu.SemaphoreType.DMA((9,))],
        compiler_params=WIDE,
    )(*arrays)


def middle_kernel(got_ref, out_ref):
    base = got_ref[0, : 2 * BANK]
    dots = got_ref[0, 2 * BANK + 3 * GROUP :]
    for x in range(1, NX):
        base += got_ref[x, : 2 * BANK]
        dots += got_ref[x, 2 * BANK + 3 * GROUP :]
    base = jnp.transpose(base)
    rights = []
    for kind in range(3):
        start = 2 * BANK + kind * GROUP
        rights += [got_ref[x, start : start + GROUP] for x in range(NX)]
    rights.append(jnp.zeros((2 * BANK - 3 * NX * GROUP, CHUNK), f32))
    rights = jnp.transpose(jnp.concatenate(rights, axis=0))
    for yh in range(NYH):
        out_ref[yh, :OWN] = base[yh * OWN : (yh + 1) * OWN]
        out_ref[yh, OWN : 2 * OWN] = rights[yh * OWN : (yh + 1) * OWN]
        out_ref[yh, 2 * OWN + 8 :] = jnp.zeros((8, 2 * BANK), f32)
        for k in range(CHUNKS):
            line = 2 * OWN + 8 * (k // 4)
            lane = (k % 4) * CHUNK
            out_ref[yh, line : line + 8, lane : lane + CHUNK] = dots[8 * k : 8 * k + 8]


def middle(got):
    return pl.pallas_call(
        middle_kernel,
        out_shape=jax.ShapeDtypeStruct((NYH, 2 * OWN + 16, 2 * BANK), f32),
        compiler_params=PARAMS,
    )(got)


def columns_kernel(place_ref, down_ref, right_ref, *out_refs):
    member = lax.broadcasted_iota(jnp.int32, (MEMBERS, CHUNK), 0)
    lane = lax.broadcasted_iota(jnp.int32, (MEMBERS, CHUNK), 1)
    quarter = BLOCK_MEMBERS
    row = sum((lane >= k * quarter).astype(jnp.int32) for k in range(1, NZH))
    wanted = lane + row * (NX * NC - 1) * quarter
    right = right_ref[...]
    for out_ref in out_refs:
        out_ref[:, :UNITS] = down_ref[...]
    for k in range(NX):
        start = (lax.rem(place_ref[0] + k, NX) * NC + place_ref[2]) * quarter
        chosen = member == jnp.where(lane < NZH * quarter, wanted + start, MEMBERS)
        chosen = jnp.dot(
            right, chosen.astype(f32).astype(bf16), preferred_element_type=f32
        ).astype(bf16)
        if k == 2:
            for out_ref in out_refs[1:]:
                out_ref[:, KEPT:] = chosen
        else:
            out_refs[(0, 1, None, 2)[k]][:, UNITS:KEPT] = chosen


def down_columns(place, down, right):
    own = jax.ShapeDtypeStruct((WIDTH, KEPT), bf16)
    leaving = jax.ShapeDtypeStruct((WIDTH, KEPT + CHUNK), bf16)
    return pl.pallas_call(
        columns_kernel,
        out_shape=[own, leaving, leaving],
        in_specs=[SMEM, VMEM, VMEM],
        compiler_params=PARAMS,
    )(place, down, right)


def hidden_kernel(ids_ref, got_ref, out_ref, hidden_ref, down_ref):
    base = got_ref[0, :OWN]
    all_dots = got_ref[0, 2 * OWN :]
    for yh in range(1, NYH):
        base += got_ref[yh, :OWN]
        all_dots += got_ref[yh, 2 * OWN :]
    along = NX * GROUP
    rights = [
        jnp.concatenate(
            [
                got_ref[yh, OWN : 2 * OWN, kind * along : (kind + 1) * along]
                for yh in range(NYH)
            ],
            axis=1,
        )
        for kind in range(3)
    ]
    rights = jnp.concatenate(rights, axis=0).astype(bf16)
    step = CHUNK * TOKENS
    scale = f32(1.0 / math.sqrt(D))
    base = jnp.concatenate([base[:, :BANK], base[:, BANK:]], axis=0)
    base = jnp.concatenate(split_three(base), axis=0)
    repeat = (
        lax.broadcasted_iota(jnp.int32, (CHUNK, step), 1) // TOKENS
        == lax.broadcasted_iota(jnp.int32, (CHUNK, step), 0)
    ).astype(f32).astype(bf16)
    token = lax.broadcasted_iota(jnp.int32, (1, step), 1) % TOKENS
    for part in range(CHUNKS):
        rows = slice(part * step, (part + 1) * step)
        chosen = (
            lax.broadcasted_iota(jnp.int32, (BANK, step), 0) == ids_ref[:, rows]
        ).astype(f32).astype(bf16)
        picked = jnp.dot(base, chosen, preferred_element_type=f32)
        picked = picked[: 2 * OWN] + picked[2 * OWN : 4 * OWN] + picked[4 * OWN :]
        line, lane = 8 * (part // 4), (part % 4) * CHUNK
        dots = all_dots[line : line + 8, lane : lane + CHUNK]
        dots = jnp.concatenate(split_three(dots), axis=0)
        dots = jnp.dot(dots, repeat, preferred_element_type=f32)
        dots = (dots[:8] + dots[8:16] + dots[16:]) * scale
        right = jnp.dot(
            rights[:, part * CHUNK : (part + 1) * CHUNK], repeat, preferred_element_type=f32
        )
        gate_dot = jnp.zeros((1, step), f32)
        up_dot = jnp.zeros((1, step), f32)
        for j in range(TOKENS):
            gate_dot = jnp.where(token == j, dots[j : j + 1], gate_dot)
            up_dot = jnp.where(token == j, dots[TOKENS + j : TOKENS + j + 1], up_dot)
        gate_pre = picked[:OWN] + spread * gate_dot * right[:OWN]
        up_pre = picked[OWN:] + spread * up_dot * right[OWN : 2 * OWN]
        hidden = (gate_pre / (1.0 + jnp.exp(-gate_pre)) * up_pre).astype(bf16)
        hidden_ref[:, rows] = hidden
        down_ref[:, rows] = jnp.sum(
            hidden.astype(f32) * right[2 * OWN :], axis=0, keepdims=True
        )
    line = lax.broadcasted_iota(jnp.int32, (OWN, REST), 0)
    for x in range(NX):
        for c in range(NC):
            starts = [((x * NZH + zh) * NC + c) * BLOCK for zh in range(NZH)]
            dots = jnp.concatenate([down_ref[:, k : k + BLOCK] for k in starts], axis=1)
            down = jnp.zeros((OWN, REST), f32)
            for k in range(PART // REST):
                piece = dots[:, k * REST : (k + 1) * REST]
                high = piece.astype(bf16).astype(f32)
                down = jnp.where(line == k, high, down)
                down = jnp.where(line == k + 8, piece - high, down)
            block = jnp.concatenate(
                [hidden_ref[:, k : k + BLOCK].astype(f32) for k in starts] + [down], axis=1
            ).astype(bf16)
            for yh in range(NYH):
                out_ref[c, x, yh] = block


def activate(ids, got):
    return pl.pallas_call(
        hidden_kernel,
        out_shape=jax.ShapeDtypeStruct((NC, NX, NYH, OWN, PADDED), bf16),
        scratch_shapes=[pltpu.VMEM((OWN, ROWS), bf16), pltpu.VMEM((1, ROWS), f32)],
        compiler_params=PARAMS,
    )(ids, got)


def project_kernel(place_ref, hidden_hbm, *refs):
    out_ref, own_ref, other_ref, right_ref = refs[10:14]
    arrived, hidden_ref = refs[14:16]
    parts = [pl.ds(k * CHUNK, CHUNK) for k in range(8)]
    rows = fetch(
        [hidden_hbm.at[part] for part in parts],
        [hidden_ref.at[part] for part in parts],
        arrived.at[3],
    )
    half = WIDTH // 2
    places = [(0, WIDTH), (WIDTH, WIDTH), (2 * WIDTH, half), (2 * WIDTH + half, half)]
    places = [pl.ds(*spot) for spot in places + [(3 * WIDTH, WIDTH)]]
    lanes = [slice(UNITS, KEPT)] * 2 + [slice(KEPT, KEPT + CHUNK)] * 2 + [slice(UNITS, KEPT)]
    copies = [
        fetch(
            [ref.at[:, :UNITS] for ref in refs[:5]],
            [own_ref.at[spot] for spot in places],
            arrived.at[0],
        ),
        fetch(
            [ref.at[:, lane] for ref, lane in zip(refs[:5], lanes)],
            [right_ref.at[spot] for spot in places],
            arrived.at[1],
        ),
        fetch(
            [ref.at[:, :UNITS] for ref in refs[5:10]],
            [other_ref.at[spot] for spot in places],
            arrived.at[2],
        ),
    ]
    x_here, c_here = place_ref[0], place_ref[2]
    for copy in rows:
        copy.wait()
    dots = jnp.zeros((16, CHUNK), f32)
    for source in range(NC * NX * NYH):
        dots += hidden_ref[source * OWN : source * OWN + 16, PADDED - CHUNK :].astype(f32)
    dots = dots[:8] + dots[8:]
    eye = lax.broadcasted_iota(jnp.int32, (REST, REST), 0) == lax.broadcasted_iota(
        jnp.int32, (REST, REST), 1
    )
    columns = []
    for k in range(PART // REST):
        row = dots[k : k + 1, CHUNK - REST :]
        columns.append(jnp.sum(jnp.where(eye, row, 0.0), axis=1, keepdims=True))
    dot = jnp.concatenate(columns, axis=0) * f32(spread / math.sqrt(FF))
    own_member = (
        lax.broadcasted_iota(jnp.int32, (PART, CHUNK), 0) // TOKENS
        == lax.broadcasted_iota(jnp.int32, (PART, CHUNK), 1)
    )
    shares = jnp.where(own_member, dot, 0.0)
    high = shares.astype(bf16)
    low = (shares - high.astype(f32)).astype(bf16)
    shares = jnp.concatenate([high, low], axis=1)
    start = pl.multiple_of(c_here * UNITS, UNITS)
    own_rows = hidden_ref[pl.ds(start, UNITS), :].astype(f32)
    start = pl.multiple_of((1 - c_here) * UNITS, UNITS)
    other_rows = hidden_ref[pl.ds(start, UNITS), :].astype(f32)
    own_rows = jnp.transpose(own_rows)[:PART].astype(bf16)
    other_rows = jnp.transpose(other_rows)[:PART].astype(bf16)
    for copy in copies[0]:
        copy.wait()
    total = lax.dot_general(own_rows, own_ref[...], NT, preferred_element_type=f32)
    for copy in copies[1]:
        copy.wait()
    right = right_ref[...]
    right = jnp.concatenate([right, right], axis=1)
    total += lax.dot_general(shares, right, NT, preferred_element_type=f32)
    for copy in copies[2]:
        copy.wait()
    total += lax.dot_general(other_rows, other_ref[...], NT, preferred_element_type=f32)
    for k in range(NX):
        x = lax.rem(x_here - k + NX, NX)
        part = total[:, k * WIDTH : (k + 1) * WIDTH]
        for zh in range(NZH):
            top = part[zh * BLOCK : zh * BLOCK + BLOCK // 2]
            bottom = part[zh * BLOCK + BLOCK // 2 : (zh + 1) * BLOCK]
            out_ref[zh * NX + x] = jnp.concatenate([top, bottom], axis=1).astype(bf16)


def project(place, hidden, own, other):
    return pl.pallas_call(
        project_kernel,
        out_shape=jax.ShapeDtypeStruct((NZH * NX, BLOCK // 2, 2 * WIDTH), bf16),
        in_specs=[SMEM] + [HBM] * 11,
        scratch_shapes=[pltpu.VMEM((NX * WIDTH, UNITS), bf16)] * 2
        + [pltpu.VMEM((NX * WIDTH, CHUNK), bf16), pltpu.SemaphoreType.DMA((4, 8))]
        + [pltpu.VMEM((NC * UNITS, PADDED), bf16)],
        compiler_params=WIDE,
    )(place, hidden, *own, *other)


def loss_kernel(place_ref, got_ref, target_ref, raw_ref, out_ref):
    total = got_ref[0].astype(f32)
    for source in range(1, NZH * NX):
        total += got_ref[source].astype(f32)
    raw = jnp.concatenate([total[:, :WIDTH], total[:, WIDTH:]], axis=0)
    raw_ref[...] = raw
    error = raw - target_ref[...].astype(f32)
    squares = jnp.sum(error * error, axis=1, keepdims=True)
    member = (
        lax.broadcasted_iota(jnp.int32, (BLOCK, CHUNK), 0) // TOKENS
        + place_ref[3] * BLOCK_MEMBERS
        - lax.broadcasted_iota(jnp.int32, (BLOCK, CHUNK), 1)
    )
    line = lax.broadcasted_iota(jnp.int32, (8, CHUNK), 0)
    placed = jnp.zeros((8, CHUNK), f32)
    for k in range(CHUNKS):
        here = jnp.sum(jnp.where(member == k * CHUNK, squares, 0.0), axis=0, keepdims=True)
        placed = jnp.where(line == k, here, placed)
    for k in range(NYH * NZL * NYL):
        out_ref[k] = placed


def piece_losses(place, got, target):
    return pl.pallas_call(
        loss_kernel,
        out_shape=[
            jax.ShapeDtypeStruct((BLOCK, WIDTH), f32),
            jax.ShapeDtypeStruct((NYH * NZL * NYL, 8, CHUNK), f32),
        ],
        in_specs=[SMEM] + [VMEM] * 2,
        compiler_params=PARAMS,
    )(place, got, target)


def update_kernel(place_ref, far_ref, *refs):
    left_hbm, blocks = refs[:3], refs[3:7]
    out_hbm, factor_ref, left_refs = refs[7:10], refs[10], refs[11:14]
    out_refs, arrived, left_sem = refs[14:17], refs[17], refs[18]
    copies = fetch(left_hbm, left_refs, arrived)
    leaving = []
    x_here = place_ref[0]
    group = NYH * GROUP
    for kind in range(3):
        for k, block in enumerate(blocks):
            start = pl.multiple_of(lax.rem(x_here - k + NX, NX) * group, group)
            factor_ref[kind, pl.ds(start, group), :] = block[kind]
    losses = far_ref[0]
    for source in range(1, NX * NC * NZH):
        losses += far_ref[source]
    losses = losses * f32(1.0 / (TOKENS * D))
    valid = lax.broadcasted_iota(jnp.int32, (8, CHUNK), 0) < CHUNKS
    mean = jnp.sum(losses, keepdims=True) * f32(1.0 / MEMBERS)
    offset = jnp.where(valid, losses - mean, 0.0)
    variance = jnp.sum(offset * offset, keepdims=True) * f32(1.0 / MEMBERS)
    weights = -offset / jnp.sqrt(variance + epsilon) * f32(1.0 / math.sqrt(MEMBERS))
    weights = jnp.concatenate([weights[k : k + 1] for k in range(CHUNKS)], axis=1)
    for kind in range(3):
        copies[kind].wait()
        scaled = left_refs[kind][...].astype(f32) * weights
        high = scaled.astype(bf16)
        low = (scaled - high.astype(f32)).astype(bf16)
        for part in range(2):
            lines = slice(part * (WIDTH // 2), (part + 1) * (WIDTH // 2))
            out_refs[kind][lines] = jnp.dot(
                high[lines], factor_ref[kind], preferred_element_type=f32
            ) + jnp.dot(low[lines], factor_ref[kind], preferred_element_type=f32)
            copy = pltpu.make_async_copy(
                out_refs[kind].at[lines], out_hbm[kind].at[lines], left_sem.at[2 * kind + part]
            )
            copy.start()
            leaving.append(copy)
    for copy in leaving:
        copy.wait()


def updates(place, far, lefts, blocks):
    out = jax.ShapeDtypeStruct((WIDTH, UNITS), f32)
    return pl.pallas_call(
        update_kernel,
        out_shape=[out] * 3,
        in_specs=[SMEM, VMEM] + [HBM] * 3 + [VMEM] * NX,
        out_specs=[HBM] * 3,
        scratch_shapes=[pltpu.VMEM((3, MEMBERS, UNITS), bf16)]
        + [pltpu.VMEM((WIDTH, MEMBERS), bf16)] * 3
        + [pltpu.VMEM((WIDTH, UNITS), f32)] * 3
        + [pltpu.SemaphoreType.DMA((3,)), pltpu.SemaphoreType.DMA((6,))],
        compiler_params=PARAMS,
    )(place, far, *lefts, *blocks)


def after(earlier, *arrays):
    return lax.optimization_barrier((earlier, *arrays))[1:]


def shifted(value, axis, size, k):
    return lax.ppermute(value, axis, [(i, (i + k) % size) for i in range(size)])


def per_device(
    states,
    token_ids,
    gate_matrix,
    up_matrix,
    down_matrix,
    gate_left,
    gate_right,
    up_left,
    up_right,
    down_left,
    down_right,
    target,
):
    x_index, yh_index, c_index = (lax.axis_index(axis) for axis in ("x", "yh", "c"))
    block = (lax.axis_index("zh") * NX + x_index) * NC + c_index
    place = jnp.stack([x_index, yh_index, c_index, block]).astype(jnp.int32)
    forth = to_owner()
    back = [(b, a) for a, b in forth]

    columns = down_columns(place, down_matrix.T, down_right.T)

    got, own_factors = front(
        token_ids.T,
        states.T,
        gate_left.T,
        up_left.T,
        gate_matrix,
        up_matrix,
        gate_right,
        up_right,
        down_left,
    )
    along = [shifted(own_factors, "yh", NYH, k) for k in (1, 2, 3)]
    sent = middle(lax.all_to_all(got, "x", 0, 0))
    sent, along, columns = lax.optimization_barrier((sent, along, columns))
    got = lax.all_to_all(sent, "yh", 0, 0)

    before = shifted(columns[1], "x", NX, 1)
    later = shifted(columns[2], "x", NX, 3)
    partner = shifted(columns[0], "c", NC, 1)
    (target,) = after(sent, target)
    piece_target = lax.ppermute(target, EVERY, back)
    ids = token_ids.reshape(NX, NYH, GROUP * TOKENS).transpose(1, 0, 2).reshape(1, ROWS)
    outgoing = activate(ids, got)
    outgoing, before, later, partner, piece_target = lax.optimization_barrier(
        (outgoing, before, later, partner, piece_target)
    )

    hidden = lax.all_to_all(
        outgoing.reshape(NC * NX * NYH * OWN, PADDED), ("c", "x", "yh"), 0, 0, tiled=True
    )
    half = WIDTH // 2
    ahead = shifted(before[:half], "x", NX, 1)
    behind = shifted(later[half:], "x", NX, 3)
    columns = [columns[0], before, ahead, behind, later]
    others = [partner] + [shifted(column, "c", NC, 1) for column in columns[1:]]

    pieces = project(place, hidden, columns, others)
    (along,) = after(hidden, along)
    got = lax.all_to_all(pieces, ("zh", "zl", "yl"), 0, 0)
    around = jnp.stack([own_factors] + along).reshape(NYH, 3, GROUP, UNITS)
    around = jnp.concatenate(
        [
            lax.dynamic_index_in_dim(around, lax.rem(yh_index - k + NYH, NYH), 0, keepdims=False)
            for k in range(NYH)
        ],
        axis=1,
    )
    arounds = [shifted(around, "x", NX, k) for k in (1, 2, 3)]
    raw, sent = piece_losses(place, got, piece_target)
    raw_out = lax.ppermute(raw, EVERY, forth)

    near = lax.all_to_all(sent, ("yh", "zl", "yl"), 0, 0)
    near = jnp.broadcast_to(jnp.sum(near, axis=0), (NX * NC * NZH, 8, CHUNK))
    near, arounds = lax.optimization_barrier((near, arounds))
    far = lax.all_to_all(near, ("x", "c", "zh"), 0, 0)
    gate_update, up_update, down_update = updates(
        place,
        far,
        (gate_left.T, up_left.T, down_right.T),
        (around, *arounds),
    )
    return (raw_out, gate_update, up_update, down_update.T)


def solution(mesh):
    cut = Mesh(mesh.devices.reshape(NX, NYH, NZH, NZL, NYL, NC), EVERY)
    return jax.shard_map(
        per_device,
        mesh=cut,
        in_specs=(
            P(None, POP),
            P(),
            P(POP, TP),
            P(POP, TP),
            P(TP, POP),
            P(None, POP),
            P(POP, TP),
            P(None, POP),
            P(POP, TP),
            P(POP, TP),
            P(None, POP),
            P(TP, POP),
        ),
        out_specs=(P(TP, POP), P(POP, TP), P(POP, TP), P(TP, POP)),
        check_vma=False,
    )
```

```python
import math

import jax
import jax.numpy as jnp
from jax import lax
from jax.experimental import pallas as pl
from jax.experimental.pallas import tpu as pltpu
from jax.sharding import Mesh, PartitionSpec as P

D = 5120
FF = 16384
MEMBERS = 640
TOKENS = 4
ROWS = MEMBERS * TOKENS
BANK = 256

spread = 0.5
epsilon = 1e-06

f32 = jnp.float32
bf16 = jnp.bfloat16

NX, NYH, NZH, NZL, NYL, NC = 4, 4, 4, 2, 2, 2
POP = ("x", "yh")
TP = ("zh", "zl", "yl", "c")
EVERY = POP + TP
GROUP = MEMBERS // (NX * NYH)
UNITS = 512
OWN = UNITS // (NX * NYH)
WIDTH = D // (NX * NYH)
CHUNK = 128
CHUNKS = MEMBERS // CHUNK
PART = ROWS // (NX * NC)
BLOCK = ROWS // (NZH * NZL * NYL * NC)
BLOCK_MEMBERS = BLOCK // TOKENS
PADDED = 384
REST = PADDED - PART
KEPT = UNITS + CHUNK


def to_owner():
    pairs = []
    for x in range(NX):
        for yh in range(NYH):
            for zh in range(NZH):
                for column in range(NZL * NYL):
                    for c in range(NC):
                        here = (x * NYH + yh) * 32 + (zh * 4 + column) * NC + c
                        row = (zh * NX + x) * NC + c
                        pairs.append((here, (column * NYH + yh) * 32 + row))
    return pairs


def split_three(value):
    high = value.astype(bf16)
    rest = value - high.astype(f32)
    middle = rest.astype(bf16)
    low = (rest - middle.astype(f32)).astype(bf16)
    return high, middle, low


SMEM = pl.BlockSpec(memory_space=pltpu.SMEM)
VMEM = pl.BlockSpec(memory_space=pltpu.VMEM)
WIDE = pltpu.CompilerParams(vmem_limit_bytes=60 * 1024 * 1024)
HBM = pl.BlockSpec(memory_space=pltpu.HBM)
PARAMS = pltpu.CompilerParams(vmem_limit_bytes=24 * 1024 * 1024)
NT = (((1,), (1,)), ((), ()))


def fetch(sources, targets, arrived):
    copies = [
        pltpu.make_async_copy(source, target, arrived.at[k])
        for k, (source, target) in enumerate(zip(sources, targets, strict=True))
    ]
    for copy in copies:
        copy.start()
    return copies


def front_kernel(*refs):
    out_ref, factors_ref, held, arrived = refs[9], refs[10], refs[11:20], refs[20]
    copies = fetch(refs[:9], held, arrived)
    ids_ref, states_ref, gate_left_ref, up_left_ref, gate_ref, up_ref = held[:6]
    copies[0].wait()
    copies[1].wait()
    states = jnp.transpose(states_ref[...].astype(f32)).astype(bf16)
    bank = lax.broadcasted_iota(jnp.int32, (BANK, MEMBERS), 0)
    line = lax.broadcasted_iota(jnp.int32, (8, MEMBERS), 0)
    dots = jnp.zeros((8, MEMBERS), f32)
    for kind, left in enumerate((gate_left_ref, up_left_ref)):
        copies[2 + kind].wait()
        inner = jnp.dot(states, left[...], preferred_element_type=f32)
        for j in range(TOKENS):
            chosen = jnp.where(bank == ids_ref[j : j + 1, :], inner, 0.0)
            row = jnp.sum(chosen, axis=0, keepdims=True)
            dots = jnp.where(line == kind * TOKENS + j, row, dots)
    groups = [x * NYH + yh for yh in range(NYH) for x in range(NX)]
    dots = jnp.concatenate([dots[:, g * GROUP : (g + 1) * GROUP] for g in groups], axis=1)
    for kind, matrix in enumerate((gate_ref, up_ref)):
        copies[4 + kind].wait()
        part = jnp.dot(states, matrix[...], preferred_element_type=f32)
        for x in range(NX):
            out_ref[x, kind * BANK : (kind + 1) * BANK] = part[:, x * CHUNK : (x + 1) * CHUNK]
    rights = []
    for kind in range(3):
        copies[6 + kind].wait()
        rights.append(held[6 + kind][...].astype(f32))
        start = 2 * BANK + kind * GROUP
        for x in range(NX):
            out_ref[x, start : start + GROUP] = rights[kind][:, x * CHUNK : (x + 1) * CHUNK]
    factors_ref[...] = jnp.concatenate(rights, axis=0).astype(bf16)
    for x in range(NX):
        for k in range(CHUNKS):
            start = 2 * BANK + 3 * GROUP + 8 * k
            out_ref[x, start : start + 8] = dots[:, k * CHUNK : (k + 1) * CHUNK]


def front(*arrays):
    return pl.pallas_call(
        front_kernel,
        out_shape=[
            jax.ShapeDtypeStruct((NX, 2 * BANK + 4 * GROUP, CHUNK), f32),
            jax.ShapeDtypeStruct((3 * GROUP, UNITS), bf16),
        ],
        in_specs=[HBM] * 9,
        scratch_shapes=[pltpu.VMEM(array.shape, array.dtype) for array in arrays]
        + [pltpu.SemaphoreType.DMA((9,))],
        compiler_params=WIDE,
    )(*arrays)


def middle_kernel(got_ref, out_ref):
    base = got_ref[0, : 2 * BANK]
    dots = got_ref[0, 2 * BANK + 3 * GROUP :]
    for x in range(1, NX):
        base += got_ref[x, : 2 * BANK]
        dots += got_ref[x, 2 * BANK + 3 * GROUP :]
    base = jnp.transpose(base)
    rights = []
    for kind in range(3):
        start = 2 * BANK + kind * GROUP
        rights += [got_ref[x, start : start + GROUP] for x in range(NX)]
    rights.append(jnp.zeros((2 * BANK - 3 * NX * GROUP, CHUNK), f32))
    rights = jnp.transpose(jnp.concatenate(rights, axis=0))
    for yh in range(NYH):
        out_ref[yh, :OWN] = base[yh * OWN : (yh + 1) * OWN]
        out_ref[yh, OWN : 2 * OWN] = rights[yh * OWN : (yh + 1) * OWN]
        out_ref[yh, 2 * OWN + 8 :] = jnp.zeros((8, 2 * BANK), f32)
        for k in range(CHUNKS):
            line = 2 * OWN + 8 * (k // 4)
            lane = (k % 4) * CHUNK
            out_ref[yh, line : line + 8, lane : lane + CHUNK] = dots[8 * k : 8 * k + 8]


def middle(got):
    return pl.pallas_call(
        middle_kernel,
        out_shape=jax.ShapeDtypeStruct((NYH, 2 * OWN + 16, 2 * BANK), f32),
        compiler_params=PARAMS,
    )(got)


def columns_kernel(place_ref, down_ref, right_ref, *out_refs):
    member = lax.broadcasted_iota(jnp.int32, (MEMBERS, CHUNK), 0)
    lane = lax.broadcasted_iota(jnp.int32, (MEMBERS, CHUNK), 1)
    quarter = BLOCK_MEMBERS
    row = sum((lane >= k * quarter).astype(jnp.int32) for k in range(1, NZH))
    wanted = lane + row * (NX * NC - 1) * quarter
    right = right_ref[...]
    for out_ref in out_refs:
        out_ref[:, :UNITS] = down_ref[...]
    for k in range(NX):
        start = (lax.rem(place_ref[0] + k, NX) * NC + place_ref[2]) * quarter
        chosen = member == jnp.where(lane < NZH * quarter, wanted + start, MEMBERS)
        chosen = jnp.dot(
            right, chosen.astype(f32).astype(bf16), preferred_element_type=f32
        ).astype(bf16)
        if k == 2:
            for out_ref in out_refs[1:]:
                out_ref[:, KEPT:] = chosen
        else:
            out_refs[(0, 1, None, 2)[k]][:, UNITS:KEPT] = chosen


def down_columns(place, down, right):
    own = jax.ShapeDtypeStruct((WIDTH, KEPT), bf16)
    leaving = jax.ShapeDtypeStruct((WIDTH, KEPT + CHUNK), bf16)
    return pl.pallas_call(
        columns_kernel,
        out_shape=[own, leaving, leaving],
        in_specs=[SMEM, VMEM, VMEM],
        compiler_params=PARAMS,
    )(place, down, right)


def hidden_kernel(ids_ref, got_ref, out_ref, hidden_ref, down_ref):
    base = got_ref[0, :OWN]
    all_dots = got_ref[0, 2 * OWN :]
    for yh in range(1, NYH):
        base += got_ref[yh, :OWN]
        all_dots += got_ref[yh, 2 * OWN :]
    along = NX * GROUP
    rights = [
        jnp.concatenate(
            [
                got_ref[yh, OWN : 2 * OWN, kind * along : (kind + 1) * along]
                for yh in range(NYH)
            ],
            axis=1,
        )
        for kind in range(3)
    ]
    rights = jnp.concatenate(rights, axis=0).astype(bf16)
    step = CHUNK * TOKENS
    scale = f32(1.0 / math.sqrt(D))
    base = jnp.concatenate([base[:, :BANK], base[:, BANK:]], axis=0)
    base = jnp.concatenate(split_three(base), axis=0)
    repeat = (
        lax.broadcasted_iota(jnp.int32, (CHUNK, step), 1) // TOKENS
        == lax.broadcasted_iota(jnp.int32, (CHUNK, step), 0)
    ).astype(f32).astype(bf16)
    token = lax.broadcasted_iota(jnp.int32, (1, step), 1) % TOKENS
    for part in range(CHUNKS):
        rows = slice(part * step, (part + 1) * step)
        chosen = (
            lax.broadcasted_iota(jnp.int32, (BANK, step), 0) == ids_ref[:, rows]
        ).astype(f32).astype(bf16)
        picked = jnp.dot(base, chosen, preferred_element_type=f32)
        picked = picked[: 2 * OWN] + picked[2 * OWN : 4 * OWN] + picked[4 * OWN :]
        line, lane = 8 * (part // 4), (part % 4) * CHUNK
        dots = all_dots[line : line + 8, lane : lane + CHUNK]
        dots = jnp.concatenate(split_three(dots), axis=0)
        dots = jnp.dot(dots, repeat, preferred_element_type=f32)
        dots = (dots[:8] + dots[8:16] + dots[16:]) * scale
        right = jnp.dot(
            rights[:, part * CHUNK : (part + 1) * CHUNK], repeat, preferred_element_type=f32
        )
        gate_dot = jnp.zeros((1, step), f32)
        up_dot = jnp.zeros((1, step), f32)
        for j in range(TOKENS):
            gate_dot = jnp.where(token == j, dots[j : j + 1], gate_dot)
            up_dot = jnp.where(token == j, dots[TOKENS + j : TOKENS + j + 1], up_dot)
        gate_pre = picked[:OWN] + spread * gate_dot * right[:OWN]
        up_pre = picked[OWN:] + spread * up_dot * right[OWN : 2 * OWN]
        hidden = (gate_pre / (1.0 + jnp.exp(-gate_pre)) * up_pre).astype(bf16)
        hidden_ref[:, rows] = hidden
        down_ref[:, rows] = jnp.sum(
            hidden.astype(f32) * right[2 * OWN :], axis=0, keepdims=True
        )
    line = lax.broadcasted_iota(jnp.int32, (OWN, REST), 0)
    for x in range(NX):
        for c in range(NC):
            starts = [((x * NZH + zh) * NC + c) * BLOCK for zh in range(NZH)]
            dots = jnp.concatenate([down_ref[:, k : k + BLOCK] for k in starts], axis=1)
            down = jnp.zeros((OWN, REST), f32)
            for k in range(PART // REST):
                piece = dots[:, k * REST : (k + 1) * REST]
                high = piece.astype(bf16).astype(f32)
                down = jnp.where(line == k, high, down)
                down = jnp.where(line == k + 8, piece - high, down)
            block = jnp.concatenate(
                [hidden_ref[:, k : k + BLOCK].astype(f32) for k in starts] + [down], axis=1
            ).astype(bf16)
            for yh in range(NYH):
                out_ref[c, x, yh] = block


def activate(ids, got):
    return pl.pallas_call(
        hidden_kernel,
        out_shape=jax.ShapeDtypeStruct((NC, NX, NYH, OWN, PADDED), bf16),
        scratch_shapes=[pltpu.VMEM((OWN, ROWS), bf16), pltpu.VMEM((1, ROWS), f32)],
        compiler_params=PARAMS,
    )(ids, got)


def project_kernel(place_ref, hidden_hbm, *refs):
    out_ref, own_ref, other_ref, right_ref = refs[10:14]
    arrived, hidden_ref = refs[14:16]
    parts = [pl.ds(k * UNITS, UNITS) for k in range(NC)]
    rows = fetch(
        [hidden_hbm.at[part] for part in parts],
        [hidden_ref.at[part] for part in parts],
        arrived.at[3],
    )
    half = WIDTH // 2
    places = [(0, WIDTH), (WIDTH, WIDTH), (2 * WIDTH, half), (2 * WIDTH + half, half)]
    places = [pl.ds(*spot) for spot in places + [(3 * WIDTH, WIDTH)]]
    lanes = [slice(UNITS, KEPT)] * 2 + [slice(KEPT, KEPT + CHUNK)] * 2 + [slice(UNITS, KEPT)]
    copies = [
        fetch(
            [ref.at[:, :UNITS] for ref in refs[:5]],
            [own_ref.at[spot] for spot in places],
            arrived.at[0],
        ),
        fetch(
            [ref.at[:, lane] for ref, lane in zip(refs[:5], lanes)],
            [right_ref.at[spot] for spot in places],
            arrived.at[1],
        ),
        fetch(
            [ref.at[:, :UNITS] for ref in refs[5:10]],
            [other_ref.at[spot] for spot in places],
            arrived.at[2],
        ),
    ]
    x_here, c_here = place_ref[0], place_ref[2]
    for copy in rows:
        copy.wait()
    dots = jnp.zeros((16, CHUNK), f32)
    for source in range(NC * NX * NYH):
        dots += hidden_ref[source * OWN : source * OWN + 16, PADDED - CHUNK :].astype(f32)
    dots = dots[:8] + dots[8:]
    eye = lax.broadcasted_iota(jnp.int32, (REST, REST), 0) == lax.broadcasted_iota(
        jnp.int32, (REST, REST), 1
    )
    columns = []
    for k in range(PART // REST):
        row = dots[k : k + 1, CHUNK - REST :]
        columns.append(jnp.sum(jnp.where(eye, row, 0.0), axis=1, keepdims=True))
    dot = jnp.concatenate(columns, axis=0) * f32(spread / math.sqrt(FF))
    own_member = (
        lax.broadcasted_iota(jnp.int32, (PART, CHUNK), 0) // TOKENS
        == lax.broadcasted_iota(jnp.int32, (PART, CHUNK), 1)
    )
    shares = jnp.where(own_member, dot, 0.0)
    high = shares.astype(bf16)
    low = (shares - high.astype(f32)).astype(bf16)
    shares = jnp.concatenate([high, low], axis=1)
    start = pl.multiple_of(c_here * UNITS, UNITS)
    own_rows = hidden_ref[pl.ds(start, UNITS), :].astype(f32)
    start = pl.multiple_of((1 - c_here) * UNITS, UNITS)
    other_rows = hidden_ref[pl.ds(start, UNITS), :].astype(f32)
    own_rows = jnp.transpose(own_rows)[:PART].astype(bf16)
    other_rows = jnp.transpose(other_rows)[:PART].astype(bf16)
    for copy in copies[0]:
        copy.wait()
    total = lax.dot_general(own_rows, own_ref[...], NT, preferred_element_type=f32)
    for copy in copies[1]:
        copy.wait()
    right = right_ref[...]
    right = jnp.concatenate([right, right], axis=1)
    total += lax.dot_general(shares, right, NT, preferred_element_type=f32)
    for copy in copies[2]:
        copy.wait()
    total += lax.dot_general(other_rows, other_ref[...], NT, preferred_element_type=f32)
    for k in range(NX):
        x = lax.rem(x_here - k + NX, NX)
        part = total[:, k * WIDTH : (k + 1) * WIDTH]
        for zh in range(NZH):
            top = part[zh * BLOCK : zh * BLOCK + BLOCK // 2]
            bottom = part[zh * BLOCK + BLOCK // 2 : (zh + 1) * BLOCK]
            out_ref[zh * NX + x] = jnp.concatenate([top, bottom], axis=1).astype(bf16)


def project(place, hidden, own, other):
    return pl.pallas_call(
        project_kernel,
        out_shape=jax.ShapeDtypeStruct((NZH * NX, BLOCK // 2, 2 * WIDTH), bf16),
        in_specs=[SMEM] + [HBM] * 11,
        scratch_shapes=[pltpu.VMEM((NX * WIDTH, UNITS), bf16)] * 2
        + [pltpu.VMEM((NX * WIDTH, CHUNK), bf16), pltpu.SemaphoreType.DMA((4, 8))]
        + [pltpu.VMEM((NC * UNITS, PADDED), bf16)],
        compiler_params=WIDE,
    )(place, hidden, *own, *other)


def loss_kernel(place_ref, got_ref, target_ref, raw_ref, out_ref):
    total = got_ref[0].astype(f32)
    for source in range(1, NZH * NX):
        total += got_ref[source].astype(f32)
    raw = jnp.concatenate([total[:, :WIDTH], total[:, WIDTH:]], axis=0)
    raw_ref[...] = raw
    error = raw - target_ref[...].astype(f32)
    squares = jnp.sum(error * error, axis=1, keepdims=True)
    member = (
        lax.broadcasted_iota(jnp.int32, (BLOCK, CHUNK), 0) // TOKENS
        + place_ref[3] * BLOCK_MEMBERS
        - lax.broadcasted_iota(jnp.int32, (BLOCK, CHUNK), 1)
    )
    line = lax.broadcasted_iota(jnp.int32, (8, CHUNK), 0)
    placed = jnp.zeros((8, CHUNK), f32)
    for k in range(CHUNKS):
        here = jnp.sum(jnp.where(member == k * CHUNK, squares, 0.0), axis=0, keepdims=True)
        placed = jnp.where(line == k, here, placed)
    for k in range(NYH * NZL * NYL):
        out_ref[k] = placed


def piece_losses(place, got, target):
    return pl.pallas_call(
        loss_kernel,
        out_shape=[
            jax.ShapeDtypeStruct((BLOCK, WIDTH), f32),
            jax.ShapeDtypeStruct((NYH * NZL * NYL, 8, CHUNK), f32),
        ],
        in_specs=[SMEM] + [VMEM] * 2,
        compiler_params=PARAMS,
    )(place, got, target)


def update_kernel(place_ref, far_ref, *refs):
    left_hbm, blocks = refs[:3], refs[3:7]
    out_hbm, factor_ref, left_refs = refs[7:10], refs[10], refs[11:14]
    out_refs, arrived, left_sem = refs[14:17], refs[17], refs[18]
    copies = fetch(left_hbm, left_refs, arrived)
    leaving = []
    x_here = place_ref[0]
    group = NYH * GROUP
    for kind in range(3):
        for k, block in enumerate(blocks):
            start = pl.multiple_of(lax.rem(x_here - k + NX, NX) * group, group)
            factor_ref[kind, pl.ds(start, group), :] = block[kind]
    losses = far_ref[0]
    for source in range(1, NX * NC * NZH):
        losses += far_ref[source]
    losses = losses * f32(1.0 / (TOKENS * D))
    valid = lax.broadcasted_iota(jnp.int32, (8, CHUNK), 0) < CHUNKS
    mean = jnp.sum(losses, keepdims=True) * f32(1.0 / MEMBERS)
    offset = jnp.where(valid, losses - mean, 0.0)
    variance = jnp.sum(offset * offset, keepdims=True) * f32(1.0 / MEMBERS)
    weights = -offset / jnp.sqrt(variance + epsilon) * f32(1.0 / math.sqrt(MEMBERS))
    weights = jnp.concatenate([weights[k : k + 1] for k in range(CHUNKS)], axis=1)
    for kind in range(3):
        copies[kind].wait()
        scaled = left_refs[kind][...].astype(f32) * weights
        high = scaled.astype(bf16)
        low = (scaled - high.astype(f32)).astype(bf16)
        for part in range(2):
            lines = slice(part * (WIDTH // 2), (part + 1) * (WIDTH // 2))
            out_refs[kind][lines] = jnp.dot(
                high[lines], factor_ref[kind], preferred_element_type=f32
            ) + jnp.dot(low[lines], factor_ref[kind], preferred_element_type=f32)
            copy = pltpu.make_async_copy(
                out_refs[kind].at[lines], out_hbm[kind].at[lines], left_sem.at[2 * kind + part]
            )
            copy.start()
            leaving.append(copy)
    for copy in leaving:
        copy.wait()


def updates(place, far, lefts, blocks):
    out = jax.ShapeDtypeStruct((WIDTH, UNITS), f32)
    return pl.pallas_call(
        update_kernel,
        out_shape=[out] * 3,
        in_specs=[SMEM, VMEM] + [HBM] * 3 + [VMEM] * NX,
        out_specs=[HBM] * 3,
        scratch_shapes=[pltpu.VMEM((3, MEMBERS, UNITS), bf16)]
        + [pltpu.VMEM((WIDTH, MEMBERS), bf16)] * 3
        + [pltpu.VMEM((WIDTH, UNITS), f32)] * 3
        + [pltpu.SemaphoreType.DMA((3,)), pltpu.SemaphoreType.DMA((6,))],
        compiler_params=PARAMS,
    )(place, far, *lefts, *blocks)


def after(earlier, *arrays):
    return lax.optimization_barrier((earlier, *arrays))[1:]


def shifted(value, axis, size, k):
    return lax.ppermute(value, axis, [(i, (i + k) % size) for i in range(size)])


def per_device(
    states,
    token_ids,
    gate_matrix,
    up_matrix,
    down_matrix,
    gate_left,
    gate_right,
    up_left,
    up_right,
    down_left,
    down_right,
    target,
):
    x_index, yh_index, c_index = (lax.axis_index(axis) for axis in ("x", "yh", "c"))
    block = (lax.axis_index("zh") * NX + x_index) * NC + c_index
    place = jnp.stack([x_index, yh_index, c_index, block]).astype(jnp.int32)
    forth = to_owner()
    back = [(b, a) for a, b in forth]

    columns = down_columns(place, down_matrix.T, down_right.T)

    got, own_factors = front(
        token_ids.T,
        states.T,
        gate_left.T,
        up_left.T,
        gate_matrix,
        up_matrix,
        gate_right,
        up_right,
        down_left,
    )
    along = [shifted(own_factors, "yh", NYH, k) for k in (1, 2, 3)]
    sent = middle(lax.all_to_all(got, "x", 0, 0))
    sent, along, columns = lax.optimization_barrier((sent, along, columns))
    got = lax.all_to_all(sent, "yh", 0, 0)

    before = shifted(columns[1], "x", NX, 1)
    later = shifted(columns[2], "x", NX, 3)
    partner = shifted(columns[0], "c", NC, 1)
    (target,) = after(sent, target)
    piece_target = lax.ppermute(target, EVERY, back)
    ids = token_ids.reshape(NX, NYH, GROUP * TOKENS).transpose(1, 0, 2).reshape(1, ROWS)
    outgoing = activate(ids, got)
    outgoing, before, later, partner, piece_target = lax.optimization_barrier(
        (outgoing, before, later, partner, piece_target)
    )

    hidden = lax.all_to_all(
        outgoing.reshape(NC * NX * NYH * OWN, PADDED), ("c", "x", "yh"), 0, 0, tiled=True
    )
    half = WIDTH // 2
    ahead = shifted(before[:half], "x", NX, 1)
    behind = shifted(later[half:], "x", NX, 3)
    columns = [columns[0], before, ahead, behind, later]
    others = [partner] + [shifted(column, "c", NC, 1) for column in columns[1:]]

    pieces = project(place, hidden, columns, others)
    (along,) = after(hidden, along)
    got = lax.all_to_all(pieces, ("zh", "zl", "yl"), 0, 0)
    around = jnp.stack([own_factors] + along).reshape(NYH, 3, GROUP, UNITS)
    around = jnp.concatenate(
        [
            lax.dynamic_index_in_dim(around, lax.rem(yh_index - k + NYH, NYH), 0, keepdims=False)
            for k in range(NYH)
        ],
        axis=1,
    )
    arounds = [shifted(around, "x", NX, k) for k in (1, 2, 3)]
    raw, sent = piece_losses(place, got, piece_target)
    raw_out = lax.ppermute(raw, EVERY, forth)

    near = lax.all_to_all(sent, ("yh", "zl", "yl"), 0, 0)
    near = jnp.broadcast_to(jnp.sum(near, axis=0), (NX * NC * NZH, 8, CHUNK))
    near, arounds = lax.optimization_barrier((near, arounds))
    far = lax.all_to_all(near, ("x", "c", "zh"), 0, 0)
    gate_update, up_update, down_update = updates(
        place,
        far,
        (gate_left.T, up_left.T, down_right.T),
        (around, *arounds),
    )
    return (raw_out, gate_update, up_update, down_update.T)


def solution(mesh):
    cut = Mesh(mesh.devices.reshape(NX, NYH, NZH, NZL, NYL, NC), EVERY)
    return jax.shard_map(
        per_device,
        mesh=cut,
        in_specs=(
            P(None, POP),
            P(),
            P(POP, TP),
            P(POP, TP),
            P(TP, POP),
            P(None, POP),
            P(POP, TP),
            P(None, POP),
            P(POP, TP),
            P(POP, TP),
            P(None, POP),
            P(TP, POP),
        ),
        out_specs=(P(TP, POP), P(POP, TP), P(POP, TP), P(TP, POP)),
        check_vma=False,
    )
```

```python
import math

import jax
import jax.numpy as jnp
from jax import lax
from jax.experimental import pallas as pl
from jax.experimental.pallas import tpu as pltpu
from jax.sharding import Mesh, PartitionSpec as P

D = 5120
FF = 16384
MEMBERS = 640
TOKENS = 4
ROWS = MEMBERS * TOKENS
BANK = 256

spread = 0.5
epsilon = 1e-06

f32 = jnp.float32
bf16 = jnp.bfloat16

NX, NYH, NZH, NZL, NYL, NC = 4, 4, 4, 2, 2, 2
POP = ("x", "yh")
TP = ("zh", "zl", "yl", "c")
EVERY = POP + TP
GROUP = MEMBERS // (NX * NYH)
UNITS = 512
OWN = UNITS // (NX * NYH)
WIDTH = D // (NX * NYH)
CHUNK = 128
CHUNKS = MEMBERS // CHUNK
PART = ROWS // (NX * NC)
BLOCK = ROWS // (NZH * NZL * NYL * NC)
BLOCK_MEMBERS = BLOCK // TOKENS
PADDED = 384
REST = PADDED - PART
KEPT = UNITS + CHUNK


def to_owner():
    pairs = []
    for x in range(NX):
        for yh in range(NYH):
            for zh in range(NZH):
                for column in range(NZL * NYL):
                    for c in range(NC):
                        here = (x * NYH + yh) * 32 + (zh * 4 + column) * NC + c
                        row = (zh * NX + x) * NC + c
                        pairs.append((here, (column * NYH + yh) * 32 + row))
    return pairs


def split_three(value):
    high = value.astype(bf16)
    rest = value - high.astype(f32)
    middle = rest.astype(bf16)
    low = (rest - middle.astype(f32)).astype(bf16)
    return high, middle, low


SMEM = pl.BlockSpec(memory_space=pltpu.SMEM)
VMEM = pl.BlockSpec(memory_space=pltpu.VMEM)
WIDE = pltpu.CompilerParams(vmem_limit_bytes=60 * 1024 * 1024)
HBM = pl.BlockSpec(memory_space=pltpu.HBM)
PARAMS = pltpu.CompilerParams(vmem_limit_bytes=24 * 1024 * 1024)
NT = (((1,), (1,)), ((), ()))


def fetch(sources, targets, arrived):
    copies = [
        pltpu.make_async_copy(source, target, arrived.at[k])
        for k, (source, target) in enumerate(zip(sources, targets, strict=True))
    ]
    for copy in copies:
        copy.start()
    return copies


def front_kernel(*refs):
    out_ref, factors_ref, held, arrived = refs[9], refs[10], refs[11:20], refs[20]
    copies = fetch(refs[:9], held, arrived)
    ids_ref, states_ref, gate_left_ref, up_left_ref, gate_ref, up_ref = held[:6]
    copies[0].wait()
    copies[1].wait()
    states = jnp.transpose(states_ref[...].astype(f32)).astype(bf16)
    bank = lax.broadcasted_iota(jnp.int32, (BANK, MEMBERS), 0)
    line = lax.broadcasted_iota(jnp.int32, (8, MEMBERS), 0)
    dots = jnp.zeros((8, MEMBERS), f32)
    for kind, left in enumerate((gate_left_ref, up_left_ref)):
        copies[2 + kind].wait()
        inner = jnp.dot(states, left[...], preferred_element_type=f32)
        for j in range(TOKENS):
            chosen = jnp.where(bank == ids_ref[j : j + 1, :], inner, 0.0)
            row = jnp.sum(chosen, axis=0, keepdims=True)
            dots = jnp.where(line == kind * TOKENS + j, row, dots)
    groups = [x * NYH + yh for yh in range(NYH) for x in range(NX)]
    dots = jnp.concatenate([dots[:, g * GROUP : (g + 1) * GROUP] for g in groups], axis=1)
    for kind, matrix in enumerate((gate_ref, up_ref)):
        copies[4 + kind].wait()
        part = jnp.dot(states, matrix[...], preferred_element_type=f32)
        for x in range(NX):
            out_ref[x, kind * BANK : (kind + 1) * BANK] = part[:, x * CHUNK : (x + 1) * CHUNK]
    rights = []
    for kind in range(3):
        copies[6 + kind].wait()
        rights.append(held[6 + kind][...].astype(f32))
        start = 2 * BANK + kind * GROUP
        for x in range(NX):
            out_ref[x, start : start + GROUP] = rights[kind][:, x * CHUNK : (x + 1) * CHUNK]
    factors_ref[...] = jnp.concatenate(rights, axis=0).astype(bf16)
    for x in range(NX):
        for k in range(CHUNKS):
            start = 2 * BANK + 3 * GROUP + 8 * k
            out_ref[x, start : start + 8] = dots[:, k * CHUNK : (k + 1) * CHUNK]


def front(*arrays):
    return pl.pallas_call(
        front_kernel,
        out_shape=[
            jax.ShapeDtypeStruct((NX, 2 * BANK + 4 * GROUP, CHUNK), f32),
            jax.ShapeDtypeStruct((3 * GROUP, UNITS), bf16),
        ],
        in_specs=[HBM] * 9,
        scratch_shapes=[pltpu.VMEM(array.shape, array.dtype) for array in arrays]
        + [pltpu.SemaphoreType.DMA((9,))],
        compiler_params=WIDE,
    )(*arrays)


def middle_kernel(got_ref, out_ref):
    base = got_ref[0, : 2 * BANK]
    dots = got_ref[0, 2 * BANK + 3 * GROUP :]
    for x in range(1, NX):
        base += got_ref[x, : 2 * BANK]
        dots += got_ref[x, 2 * BANK + 3 * GROUP :]
    base = jnp.transpose(base)
    rights = []
    for kind in range(3):
        start = 2 * BANK + kind * GROUP
        rights += [got_ref[x, start : start + GROUP] for x in range(NX)]
    rights.append(jnp.zeros((2 * BANK - 3 * NX * GROUP, CHUNK), f32))
    rights = jnp.transpose(jnp.concatenate(rights, axis=0))
    for yh in range(NYH):
        out_ref[yh, :OWN] = base[yh * OWN : (yh + 1) * OWN]
        out_ref[yh, OWN : 2 * OWN] = rights[yh * OWN : (yh + 1) * OWN]
        out_ref[yh, 2 * OWN + 8 :] = jnp.zeros((8, 2 * BANK), f32)
        for k in range(CHUNKS):
            line = 2 * OWN + 8 * (k // 4)
            lane = (k % 4) * CHUNK
            out_ref[yh, line : line + 8, lane : lane + CHUNK] = dots[8 * k : 8 * k + 8]


def middle(got):
    return pl.pallas_call(
        middle_kernel,
        out_shape=jax.ShapeDtypeStruct((NYH, 2 * OWN + 16, 2 * BANK), f32),
        compiler_params=PARAMS,
    )(got)


def columns_kernel(place_ref, down_ref, right_ref, *out_refs):
    member = lax.broadcasted_iota(jnp.int32, (MEMBERS, CHUNK), 0)
    lane = lax.broadcasted_iota(jnp.int32, (MEMBERS, CHUNK), 1)
    quarter = BLOCK_MEMBERS
    row = sum((lane >= k * quarter).astype(jnp.int32) for k in range(1, NZH))
    wanted = lane + row * (NX * NC - 1) * quarter
    right = right_ref[...]
    for out_ref in out_refs:
        out_ref[:, :UNITS] = down_ref[...]
    for k in range(NX):
        start = (lax.rem(place_ref[0] + k, NX) * NC + place_ref[2]) * quarter
        chosen = member == jnp.where(lane < NZH * quarter, wanted + start, MEMBERS)
        chosen = jnp.dot(
            right, chosen.astype(f32).astype(bf16), preferred_element_type=f32
        ).astype(bf16)
        if k == 2:
            for out_ref in out_refs[1:]:
                out_ref[:, KEPT:] = chosen
        else:
            out_refs[(0, 1, None, 2)[k]][:, UNITS:KEPT] = chosen


def down_columns(place, down, right):
    own = jax.ShapeDtypeStruct((WIDTH, KEPT), bf16)
    leaving = jax.ShapeDtypeStruct((WIDTH, KEPT + CHUNK), bf16)
    return pl.pallas_call(
        columns_kernel,
        out_shape=[own, leaving, leaving],
        in_specs=[SMEM, VMEM, VMEM],
        compiler_params=PARAMS,
    )(place, down, right)


def hidden_kernel(ids_ref, got_ref, out_ref, hidden_ref, down_ref):
    base = got_ref[0, :OWN]
    all_dots = got_ref[0, 2 * OWN :]
    for yh in range(1, NYH):
        base += got_ref[yh, :OWN]
        all_dots += got_ref[yh, 2 * OWN :]
    along = NX * GROUP
    rights = [
        jnp.concatenate(
            [
                got_ref[yh, OWN : 2 * OWN, kind * along : (kind + 1) * along]
                for yh in range(NYH)
            ],
            axis=1,
        )
        for kind in range(3)
    ]
    rights = jnp.concatenate(rights, axis=0).astype(bf16)
    step = CHUNK * TOKENS
    scale = f32(1.0 / math.sqrt(D))
    base = jnp.concatenate([base[:, :BANK], base[:, BANK:]], axis=0)
    base = jnp.concatenate(split_three(base), axis=0)
    repeat = (
        lax.broadcasted_iota(jnp.int32, (CHUNK, step), 1) // TOKENS
        == lax.broadcasted_iota(jnp.int32, (CHUNK, step), 0)
    ).astype(f32).astype(bf16)
    token = lax.broadcasted_iota(jnp.int32, (1, step), 1) % TOKENS
    for part in range(CHUNKS):
        rows = slice(part * step, (part + 1) * step)
        chosen = (
            lax.broadcasted_iota(jnp.int32, (BANK, step), 0) == ids_ref[:, rows]
        ).astype(f32).astype(bf16)
        picked = jnp.dot(base, chosen, preferred_element_type=f32)
        picked = picked[: 2 * OWN] + picked[2 * OWN : 4 * OWN] + picked[4 * OWN :]
        line, lane = 8 * (part // 4), (part % 4) * CHUNK
        dots = all_dots[line : line + 8, lane : lane + CHUNK]
        dots = jnp.concatenate(split_three(dots), axis=0)
        dots = jnp.dot(dots, repeat, preferred_element_type=f32)
        dots = (dots[:8] + dots[8:16] + dots[16:]) * scale
        right = jnp.dot(
            rights[:, part * CHUNK : (part + 1) * CHUNK], repeat, preferred_element_type=f32
        )
        gate_dot = jnp.zeros((1, step), f32)
        up_dot = jnp.zeros((1, step), f32)
        for j in range(TOKENS):
            gate_dot = jnp.where(token == j, dots[j : j + 1], gate_dot)
            up_dot = jnp.where(token == j, dots[TOKENS + j : TOKENS + j + 1], up_dot)
        gate_pre = picked[:OWN] + spread * gate_dot * right[:OWN]
        up_pre = picked[OWN:] + spread * up_dot * right[OWN : 2 * OWN]
        hidden = (gate_pre / (1.0 + jnp.exp(-gate_pre)) * up_pre).astype(bf16)
        hidden_ref[:, rows] = hidden
        down_ref[:, rows] = jnp.sum(
            hidden.astype(f32) * right[2 * OWN :], axis=0, keepdims=True
        )
    line = lax.broadcasted_iota(jnp.int32, (OWN, REST), 0)
    for x in range(NX):
        for c in range(NC):
            starts = [((x * NZH + zh) * NC + c) * BLOCK for zh in range(NZH)]
            dots = jnp.concatenate([down_ref[:, k : k + BLOCK] for k in starts], axis=1)
            down = jnp.zeros((OWN, REST), f32)
            for k in range(PART // REST):
                piece = dots[:, k * REST : (k + 1) * REST]
                high = piece.astype(bf16).astype(f32)
                down = jnp.where(line == k, high, down)
                down = jnp.where(line == k + 8, piece - high, down)
            block = jnp.concatenate(
                [hidden_ref[:, k : k + BLOCK].astype(f32) for k in starts] + [down], axis=1
            ).astype(bf16)
            for yh in range(NYH):
                out_ref[c, x, yh] = block


def activate(ids, got):
    return pl.pallas_call(
        hidden_kernel,
        out_shape=jax.ShapeDtypeStruct((NC, NX, NYH, OWN, PADDED), bf16),
        scratch_shapes=[pltpu.VMEM((OWN, ROWS), bf16), pltpu.VMEM((1, ROWS), f32)],
        compiler_params=PARAMS,
    )(ids, got)


def project_kernel(place_ref, hidden_hbm, *refs):
    out_ref, own_ref, other_ref, right_ref = refs[10:14]
    arrived, hidden_ref = refs[14:16]
    parts = [pl.ds(k * UNITS, UNITS) for k in range(NC)]
    rows = fetch(
        [hidden_hbm.at[part] for part in parts],
        [hidden_ref.at[part] for part in parts],
        arrived.at[3],
    )
    half = WIDTH // 2
    places = [(0, WIDTH), (WIDTH, WIDTH), (2 * WIDTH, half), (2 * WIDTH + half, half)]
    places = [pl.ds(*spot) for spot in places + [(3 * WIDTH, WIDTH)]]
    lanes = [slice(UNITS, KEPT)] * 2 + [slice(KEPT, KEPT + CHUNK)] * 2 + [slice(UNITS, KEPT)]
    copies = [
        fetch(
            [ref.at[:, :UNITS] for ref in refs[:5]],
            [own_ref.at[spot] for spot in places],
            arrived.at[0],
        ),
        fetch(
            [ref.at[:, lane] for ref, lane in zip(refs[:5], lanes)],
            [right_ref.at[spot] for spot in places],
            arrived.at[1],
        ),
        fetch(
            [ref.at[:, :UNITS] for ref in refs[5:10]],
            [other_ref.at[spot] for spot in places],
            arrived.at[2],
        ),
    ]
    x_here, c_here = place_ref[0], place_ref[2]
    for copy in rows:
        copy.wait()
    dots = jnp.zeros((16, CHUNK), f32)
    for source in range(NC * NX * NYH):
        dots += hidden_ref[source * OWN : source * OWN + 16, PADDED - CHUNK :].astype(f32)
    dots = dots[:8] + dots[8:]
    eye = lax.broadcasted_iota(jnp.int32, (REST, REST), 0) == lax.broadcasted_iota(
        jnp.int32, (REST, REST), 1
    )
    columns = []
    for k in range(PART // REST):
        row = dots[k : k + 1, CHUNK - REST :]
        columns.append(jnp.sum(jnp.where(eye, row, 0.0), axis=1, keepdims=True))
    dot = jnp.concatenate(columns, axis=0) * f32(spread / math.sqrt(FF))
    own_member = (
        lax.broadcasted_iota(jnp.int32, (PART, CHUNK), 0) // TOKENS
        == lax.broadcasted_iota(jnp.int32, (PART, CHUNK), 1)
    )
    shares = jnp.where(own_member, dot, 0.0)
    high = shares.astype(bf16)
    low = (shares - high.astype(f32)).astype(bf16)
    shares = jnp.concatenate([high, low], axis=1)
    start = pl.multiple_of(c_here * UNITS, UNITS)
    own_rows = hidden_ref[pl.ds(start, UNITS), :].astype(f32)
    start = pl.multiple_of((1 - c_here) * UNITS, UNITS)
    other_rows = hidden_ref[pl.ds(start, UNITS), :].astype(f32)
    own_rows = jnp.transpose(own_rows)[:PART].astype(bf16)
    other_rows = jnp.transpose(other_rows)[:PART].astype(bf16)
    for copy in copies[0]:
        copy.wait()
    total = lax.dot_general(own_rows, own_ref[...], NT, preferred_element_type=f32)
    for copy in copies[1]:
        copy.wait()
    right = right_ref[...]
    right = jnp.concatenate([right, right], axis=1)
    total += lax.dot_general(shares, right, NT, preferred_element_type=f32)
    for copy in copies[2]:
        copy.wait()
    total += lax.dot_general(other_rows, other_ref[...], NT, preferred_element_type=f32)
    for k in range(NX):
        x = lax.rem(x_here - k + NX, NX)
        part = total[:, k * WIDTH : (k + 1) * WIDTH]
        for zh in range(NZH):
            top = part[zh * BLOCK : zh * BLOCK + BLOCK // 2]
            bottom = part[zh * BLOCK + BLOCK // 2 : (zh + 1) * BLOCK]
            out_ref[zh * NX + x] = jnp.concatenate([top, bottom], axis=1).astype(bf16)


def project(place, hidden, own, other):
    return pl.pallas_call(
        project_kernel,
        out_shape=jax.ShapeDtypeStruct((NZH * NX, BLOCK // 2, 2 * WIDTH), bf16),
        in_specs=[SMEM] + [HBM] * 11,
        scratch_shapes=[pltpu.VMEM((NX * WIDTH, UNITS), bf16)] * 2
        + [pltpu.VMEM((NX * WIDTH, CHUNK), bf16), pltpu.SemaphoreType.DMA((4, 8))]
        + [pltpu.VMEM((NC * UNITS, PADDED), bf16)],
        compiler_params=WIDE,
    )(place, hidden, *own, *other)


def loss_kernel(place_ref, got_ref, target_hbm, raw_hbm, out_ref, target_ref, raw_ref, moved):
    arriving = pltpu.make_async_copy(target_hbm, target_ref, moved.at[0])
    arriving.start()
    total = got_ref[0].astype(f32)
    for source in range(1, NZH * NX):
        total += got_ref[source].astype(f32)
    raw = jnp.concatenate([total[:, :WIDTH], total[:, WIDTH:]], axis=0)
    raw_ref[...] = raw
    leaving = pltpu.make_async_copy(raw_ref, raw_hbm, moved.at[1])
    leaving.start()
    arriving.wait()
    error = raw - target_ref[...].astype(f32)
    squares = jnp.sum(error * error, axis=1, keepdims=True)
    member = (
        lax.broadcasted_iota(jnp.int32, (BLOCK, CHUNK), 0) // TOKENS
        + place_ref[3] * BLOCK_MEMBERS
        - lax.broadcasted_iota(jnp.int32, (BLOCK, CHUNK), 1)
    )
    line = lax.broadcasted_iota(jnp.int32, (8, CHUNK), 0)
    placed = jnp.zeros((8, CHUNK), f32)
    for k in range(CHUNKS):
        here = jnp.sum(jnp.where(member == k * CHUNK, squares, 0.0), axis=0, keepdims=True)
        placed = jnp.where(line == k, here, placed)
    for k in range(NYH * NZL * NYL):
        out_ref[k] = placed
    leaving.wait()


def piece_losses(place, got, target):
    return pl.pallas_call(
        loss_kernel,
        out_shape=[
            jax.ShapeDtypeStruct((BLOCK, WIDTH), f32),
            jax.ShapeDtypeStruct((NYH * NZL * NYL, 8, CHUNK), f32),
        ],
        in_specs=[SMEM, VMEM, HBM],
        out_specs=[HBM, VMEM],
        scratch_shapes=[
            pltpu.VMEM((BLOCK, WIDTH), bf16),
            pltpu.VMEM((BLOCK, WIDTH), f32),
            pltpu.SemaphoreType.DMA((2,)),
        ],
        compiler_params=PARAMS,
    )(place, got, target)


def update_kernel(place_ref, far_ref, *refs):
    left_hbm, blocks = refs[:3], refs[3:7]
    out_hbm, factor_ref, left_refs = refs[7:10], refs[10], refs[11:14]
    out_refs, arrived, left_sem = refs[14:17], refs[17], refs[18]
    copies = fetch(left_hbm, left_refs, arrived)
    leaving = []
    x_here = place_ref[0]
    group = NYH * GROUP
    for kind in range(3):
        for k, block in enumerate(blocks):
            start = pl.multiple_of(lax.rem(x_here - k + NX, NX) * group, group)
            factor_ref[kind, pl.ds(start, group), :] = block[kind]
    losses = far_ref[0]
    for source in range(1, NX * NC * NZH):
        losses += far_ref[source]
    losses = losses * f32(1.0 / (TOKENS * D))
    valid = lax.broadcasted_iota(jnp.int32, (8, CHUNK), 0) < CHUNKS
    mean = jnp.sum(losses, keepdims=True) * f32(1.0 / MEMBERS)
    offset = jnp.where(valid, losses - mean, 0.0)
    variance = jnp.sum(offset * offset, keepdims=True) * f32(1.0 / MEMBERS)
    weights = -offset / jnp.sqrt(variance + epsilon) * f32(1.0 / math.sqrt(MEMBERS))
    weights = jnp.concatenate([weights[k : k + 1] for k in range(CHUNKS)], axis=1)
    for kind in range(3):
        copies[kind].wait()
        scaled = left_refs[kind][...].astype(f32) * weights
        high = scaled.astype(bf16)
        low = (scaled - high.astype(f32)).astype(bf16)
        for part in range(2):
            lines = slice(part * (WIDTH // 2), (part + 1) * (WIDTH // 2))
            out_refs[kind][lines] = jnp.dot(
                high[lines], factor_ref[kind], preferred_element_type=f32
            ) + jnp.dot(low[lines], factor_ref[kind], preferred_element_type=f32)
            copy = pltpu.make_async_copy(
                out_refs[kind].at[lines], out_hbm[kind].at[lines], left_sem.at[2 * kind + part]
            )
            copy.start()
            leaving.append(copy)
    for copy in leaving:
        copy.wait()


def updates(place, far, lefts, blocks):
    out = jax.ShapeDtypeStruct((WIDTH, UNITS), f32)
    return pl.pallas_call(
        update_kernel,
        out_shape=[out] * 3,
        in_specs=[SMEM, VMEM] + [HBM] * 3 + [VMEM] * NX,
        out_specs=[HBM] * 3,
        scratch_shapes=[pltpu.VMEM((3, MEMBERS, UNITS), bf16)]
        + [pltpu.VMEM((WIDTH, MEMBERS), bf16)] * 3
        + [pltpu.VMEM((WIDTH, UNITS), f32)] * 3
        + [pltpu.SemaphoreType.DMA((3,)), pltpu.SemaphoreType.DMA((6,))],
        compiler_params=PARAMS,
    )(place, far, *lefts, *blocks)


def after(earlier, *arrays):
    return lax.optimization_barrier((earlier, *arrays))[1:]


def shifted(value, axis, size, k):
    return lax.ppermute(value, axis, [(i, (i + k) % size) for i in range(size)])


def per_device(
    states,
    token_ids,
    gate_matrix,
    up_matrix,
    down_matrix,
    gate_left,
    gate_right,
    up_left,
    up_right,
    down_left,
    down_right,
    target,
):
    x_index, yh_index, c_index = (lax.axis_index(axis) for axis in ("x", "yh", "c"))
    block = (lax.axis_index("zh") * NX + x_index) * NC + c_index
    place = jnp.stack([x_index, yh_index, c_index, block]).astype(jnp.int32)
    forth = to_owner()
    back = [(b, a) for a, b in forth]

    columns = down_columns(place, down_matrix.T, down_right.T)

    got, own_factors = front(
        token_ids.T,
        states.T,
        gate_left.T,
        up_left.T,
        gate_matrix,
        up_matrix,
        gate_right,
        up_right,
        down_left,
    )
    along = [shifted(own_factors, "yh", NYH, k) for k in (1, 2, 3)]
    sent = middle(lax.all_to_all(got, "x", 0, 0))
    sent, along, columns = lax.optimization_barrier((sent, along, columns))
    got = lax.all_to_all(sent, "yh", 0, 0)

    before = shifted(columns[1], "x", NX, 1)
    later = shifted(columns[2], "x", NX, 3)
    partner = shifted(columns[0], "c", NC, 1)
    (target,) = after(sent, target)
    piece_target = lax.ppermute(target, EVERY, back)
    ids = token_ids.reshape(NX, NYH, GROUP * TOKENS).transpose(1, 0, 2).reshape(1, ROWS)
    outgoing = activate(ids, got)
    outgoing, before, later, partner, piece_target = lax.optimization_barrier(
        (outgoing, before, later, partner, piece_target)
    )

    hidden = lax.all_to_all(
        outgoing.reshape(NC * NX * NYH * OWN, PADDED), ("c", "x", "yh"), 0, 0, tiled=True
    )
    half = WIDTH // 2
    ahead = shifted(before[:half], "x", NX, 1)
    behind = shifted(later[half:], "x", NX, 3)
    columns = [columns[0], before, ahead, behind, later]
    others = [partner] + [shifted(column, "c", NC, 1) for column in columns[1:]]

    pieces = project(place, hidden, columns, others)
    (along,) = after(hidden, along)
    got = lax.all_to_all(pieces, ("zh", "zl", "yl"), 0, 0)
    around = jnp.stack([own_factors] + along).reshape(NYH, 3, GROUP, UNITS)
    around = jnp.concatenate(
        [
            lax.dynamic_index_in_dim(around, lax.rem(yh_index - k + NYH, NYH), 0, keepdims=False)
            for k in range(NYH)
        ],
        axis=1,
    )
    arounds = [shifted(around, "x", NX, k) for k in (1, 2, 3)]
    raw, sent = piece_losses(place, got, piece_target)
    raw_out = lax.ppermute(raw, EVERY, forth)

    near = lax.all_to_all(sent, ("yh", "zl", "yl"), 0, 0)
    near = jnp.broadcast_to(jnp.sum(near, axis=0), (NX * NC * NZH, 8, CHUNK))
    near, arounds = lax.optimization_barrier((near, arounds))
    far = lax.all_to_all(near, ("x", "c", "zh"), 0, 0)
    gate_update, up_update, down_update = updates(
        place,
        far,
        (gate_left.T, up_left.T, down_right.T),
        (around, *arounds),
    )
    return (raw_out, gate_update, up_update, down_update.T)


def solution(mesh):
    cut = Mesh(mesh.devices.reshape(NX, NYH, NZH, NZL, NYL, NC), EVERY)
    return jax.shard_map(
        per_device,
        mesh=cut,
        in_specs=(
            P(None, POP),
            P(),
            P(POP, TP),
            P(POP, TP),
            P(TP, POP),
            P(None, POP),
            P(POP, TP),
            P(None, POP),
            P(POP, TP),
            P(POP, TP),
            P(None, POP),
            P(TP, POP),
        ),
        out_specs=(P(TP, POP), P(POP, TP), P(POP, TP), P(TP, POP)),
        check_vma=False,
    )
```
